32 devices in a mesh: dp: 8 (over z, x), head: 4 (over y, core).
Axes of the slice: x: 2, y: 2, z: 4, core: 2. Of those that a mesh axis runs over, the one named last changes fastest.
Arguments:
- queries: bfloat16 [2048, 64, 128], P('dp', 'head'), may hold values from -32 to 32
- traj_kv: bfloat16 [2048, 8, 2, 128], P('dp', 'head'), may hold values from -6 to 6
- grad_out: bfloat16 [2048, 64, 128], P('dp', 'head'), may hold values from -16 to 16
- doc_kv: bfloat16 [32, 128, 8, 2, 128], P('dp', 'head'), may hold values from -6 to 6
- citations: int32 [8, 4], replicated, may hold values from 0 to 31, as said below
- doc_slot: int32 [32], replicated, may hold values from 0 to 31, as said below
- visible_from: int32 [8, 4], P('dp'), may hold values from 0 to 3
Outputs:
- attended: bfloat16 [2048, 64, 128], P('dp', 'head')
- d_queries: bfloat16 [2048, 64, 128], P('dp', 'head')
- d_traj_kv: bfloat16 [2048, 8, 2, 128], P('dp', 'head')
- d_doc_kv: float32 [32, 128, 8, 2, 128], P('dp', 'head')
The draws below stay inside these ranges and needn't reach their ends.
Inputs may be any that keep to these rules, and one draw needn't show every extreme that they name: `citations`: each row names 4 different documents, no two of them stored on the same owner, where document d is stored on owner doc_slot[d] // 4. A permutation: document d's keys and values are row doc_slot[d] of doc_kv.
All inputs are finite; a program needn't handle non-finite values.
Results may differ from the reference program's by a relative error of at most 0.04.
Values may be sent and summed in bfloat16 or wider, within the bound.
No kernel may reach another device: no remote copies, remote signals or barrier semaphores. Data moves between devices by JAX's collectives and lax.ppermute only.
A program may use at most 192 MiB of HBM per device.

```python
import math
import jax
import jax.numpy as jnp
from jax import lax

HEADS = 64
KV_HEADS = 8
HEAD_DIM = 128
TLEN = 256
SEG = 64
DLEN = 128
DOCS_DEV = 4
NTRAJ = 8
TOKENS = 2048
CITES = 4
NDOCS = 32
NSEG = 4
N_DP = 8


def citation_plan(key):
    base = jax.random.fold_in(key, 101)
    key_slot, key_owner, key_hot, key_roll = jax.random.split(base, 4)
    slot_of = jax.random.permutation(key_slot, NDOCS).astype(jnp.int32)
    doc_at = jnp.argsort(slot_of).astype(jnp.int32)
    ranking = jax.random.randint(key_owner, (NTRAJ, N_DP), 0, 1 << 20) * N_DP + jnp.arange(N_DP, dtype=jnp.int32)[None, :]
    owners = jnp.argsort(ranking, axis=1)[:, :CITES].astype(jnp.int32)
    hot = jax.random.randint(key_hot, (N_DP,), 0, DOCS_DEV)
    roll = jax.random.randint(key_roll, (NTRAJ, CITES), 0, 10)
    hot_owner = hot[owners]
    local = jnp.where(roll < 6, hot_owner, (hot_owner + 1 + roll % (DOCS_DEV - 1)) % DOCS_DEV)
    cited = doc_at[owners * DOCS_DEV + local]
    return (slot_of, cited.astype(jnp.int32))


def draw_citations(key, part):
    return citation_plan(key)[1]


def draw_doc_slot(key, part):
    return citation_plan(key)[0]


def draw_queries(key, part):
    shape = (TOKENS, HEADS, HEAD_DIM)
    return jnp.clip(jax.random.normal(jax.random.fold_in(key, 1), shape, jnp.float32), -6.0, 6.0).astype(jnp.bfloat16)


def draw_traj_kv(key, part):
    shape = (TOKENS, KV_HEADS, 2, HEAD_DIM)
    return jnp.clip(jax.random.normal(jax.random.fold_in(key, 1), shape, jnp.float32), -6.0, 6.0).astype(jnp.bfloat16)


def set_ends(drawn, rng, low, largest):
    place = [jax.random.randint(jax.random.fold_in(rng, axis), (), 0, length) for axis, length in enumerate(drawn.shape)]
    longest = drawn.shape.index(max(drawn.shape))
    next_to = place[:longest] + [(place[longest] + 1) % drawn.shape[longest]] + place[longest + 1:]
    return drawn.at[tuple(place)].set(low).at[tuple(next_to)].set(largest)


def steps_of(own_key, dims, cuts, low, top_value):
    level, own = 1.0, jax.random.fold_in(own_key, 6)
    for dim, shards_of in cuts:
        heights = jnp.exp(jax.random.uniform(jax.random.fold_in(own, dim), (shards_of,), jnp.float32, low / len(cuts), top_value / len(cuts)))
        level = level * jnp.repeat(heights, dims[dim] // shards_of).reshape([-1 if axis == dim else 1 for axis in range(len(dims))])
    return level


def normal_values(stream_key, extent, width, most, shards=(), held_as=jnp.bfloat16):
    values = jax.random.normal(stream_key, extent, jnp.float32) * width
    if len(shards) > 0:
        values = steps_of(stream_key, extent, shards, -0.22, 0.18) * values
    return jnp.clip(values, min=-most, max=most).astype(held_as)


def setup_inputs(seed: int = 0) -> dict:
    seeds = jax.random.split(jax.random.key(seed), 8)
    return {
        "queries": draw_queries(jax.random.fold_in(seeds[7], 71), 0),
        "traj_kv": draw_traj_kv(jax.random.fold_in(seeds[7], 71), 0),
        "grad_out": normal_values(seeds[2], (TOKENS, HEADS, HEAD_DIM), 4.0, 16.0, ((0, 8), (1, 4))),
        "doc_kv": normal_values(seeds[3], (NDOCS, DLEN, KV_HEADS, 2, HEAD_DIM), 1.0, 6.0, ((0, 8), (1, 4))),
        "citations": draw_citations(jax.random.fold_in(seeds[7], 71), 0),
        "doc_slot": draw_doc_slot(jax.random.fold_in(seeds[7], 71), 0),
        "visible_from": set_ends(jax.random.randint(seeds[6], (NTRAJ, CITES), 0, NSEG), jax.random.fold_in(seeds[6], 1), 0, NSEG - 1).astype(jnp.int32),
    }


def trajectory(query, own_kv, cotangent, cited_kv, visible):
    group = HEADS // KV_HEADS
    scale = 1.0 / math.sqrt(HEAD_DIM)
    doc_keys_count = CITES * DLEN
    keys = jnp.concatenate([cited_kv[:, :, 0], own_kv[:, :, 0]], 0).astype(jnp.float32)
    value_rows = jnp.concatenate([cited_kv[:, :, 1], own_kv[:, :, 1]], 0).astype(jnp.float32)
    query_float = query.astype(jnp.float32).reshape(TLEN, KV_HEADS, group, HEAD_DIM)
    cotangent_float = cotangent.astype(jnp.float32).reshape(TLEN, KV_HEADS, group, HEAD_DIM)
    position = jnp.arange(TLEN, dtype=jnp.int32)
    segment = position // SEG
    doc_from = jnp.repeat(visible, DLEN)
    mask = jnp.concatenate([segment[:, None] >= doc_from[None, :], position[:, None] >= position[None, :]], 1)
    score = jnp.einsum('tgrd,kgd->grtk', query_float, keys) * scale
    score = jnp.where(mask[None, None], score, -jnp.inf)
    top = lax.optimization_barrier(jnp.max(score, -1, keepdims=True))
    lse = top + jnp.log(lax.optimization_barrier(jnp.sum(jnp.exp(score - top), -1, keepdims=True)))
    prob = jnp.exp(score - lse)
    prob16 = lax.optimization_barrier(prob.astype(jnp.bfloat16)).astype(jnp.float32)
    attended = jnp.einsum('grtk,kgd->tgrd', prob16, value_rows).astype(jnp.bfloat16)
    attention_float = lax.optimization_barrier(attended).astype(jnp.float32)
    output_grad_dot = jnp.einsum('kmjy,kmjy->mjk', cotangent_float, attention_float)
    dprob = jnp.einsum('tgrd,kgd->grtk', cotangent_float, value_rows)
    dscore = lax.optimization_barrier((prob * (dprob - output_grad_dot[..., None]) * scale).astype(jnp.bfloat16)).astype(jnp.float32)
    d_query = jnp.einsum('grtk,kgd->tgrd', dscore, keys).astype(jnp.bfloat16)
    key_part = jnp.einsum('grtk,tgrd->kgd', dscore, query_float)
    value_part = jnp.einsum('grtk,tgrd->kgd', prob16, cotangent_float)
    parts = jnp.stack([key_part, value_part], 2)
    own_grad = parts[doc_keys_count:].astype(jnp.bfloat16)
    doc_grad = parts[:doc_keys_count].astype(jnp.bfloat16)
    return (attended.reshape(TLEN, HEADS, HEAD_DIM), d_query.reshape(TLEN, HEADS, HEAD_DIM), own_grad, doc_grad)

def reference(queries, traj_kv, grad_out, doc_kv, citations, doc_slot, visible_from):
    slots = doc_slot[citations].astype(jnp.int32)
    query_all = queries.reshape(NTRAJ, TLEN, HEADS, HEAD_DIM)
    own_all = traj_kv.reshape(NTRAJ, TLEN, KV_HEADS, 2, HEAD_DIM)
    cot_all = grad_out.reshape(NTRAJ, TLEN, HEADS, HEAD_DIM)

    def one_step(total, item):
        query, own_kv, cotangent, slot_row, visible = item
        cited_kv = doc_kv[slot_row].reshape(CITES * DLEN, KV_HEADS, 2, HEAD_DIM)
        attended, d_query, own_grad, doc_grad = trajectory(query, own_kv, cotangent, cited_kv, visible)
        total = total.at[slot_row].add(doc_grad.astype(jnp.float32).reshape(CITES, DLEN, KV_HEADS, 2, HEAD_DIM))
        return (total, (attended, d_query, own_grad))
    start = jnp.zeros((NDOCS, DLEN, KV_HEADS, 2, HEAD_DIM), jnp.float32)
    total, (attended, d_query, own_grad) = lax.scan(one_step, start, (query_all, own_all, cot_all, slots, visible_from))
    return (attended.reshape(TOKENS, HEADS, HEAD_DIM), d_query.reshape(TOKENS, HEADS, HEAD_DIM), own_grad.reshape(TOKENS, KV_HEADS, 2, HEAD_DIM), total)
```

```python
import functools
import math

import jax
import jax.numpy as jnp
from jax import lax
from jax.experimental import pallas as pl
from jax.experimental.pallas import tpu as pltpu
from jax.sharding import PartitionSpec as P

SEG = 64
BF16 = jnp.bfloat16
F32 = jnp.float32
NT = (((1,), (1,)), ((), ()))
NN = (((1,), (0,)), ((), ()))


def dot(a, b, dims):
    return lax.dot_general(a, b, dims, preferred_element_type=F32)


def pack_kernel(docs_dev, cites, ntraj, cit_ref, slot_ref, doc_ref, out_ref, turned):
    me = lax.axis_index("dp")
    for d in range(docs_dev):
        turned[d] = jnp.swapaxes(doc_ref[d].astype(F32), 0, 1).astype(BF16)
    for t in range(ntraj):
        pick = jnp.int32(0)
        for c in range(cites):
            slot = slot_ref[cit_ref[t, c]]
            pick = jnp.where(lax.div(slot, docs_dev) == me, lax.rem(slot, docs_dev), pick)
        out_ref[t] = turned[pick]


def pack(citations, doc_slot, doc_kv, nhead):
    docs_dev, dlen_local, kv, two, hdim = doc_kv.shape
    ntraj, cites = citations.shape
    rows = kv * two
    out = pl.pallas_call(
        functools.partial(pack_kernel, docs_dev, cites, ntraj),
        out_shape=jax.ShapeDtypeStruct((ntraj, rows, dlen_local, hdim), BF16),
        in_specs=[
            pl.BlockSpec(memory_space=pltpu.SMEM),
            pl.BlockSpec(memory_space=pltpu.SMEM),
            pl.BlockSpec(memory_space=pltpu.VMEM),
        ],
        out_specs=pl.BlockSpec(memory_space=pltpu.VMEM),
        scratch_shapes=[pltpu.VMEM((docs_dev, rows, dlen_local, hdim), BF16)],
        compiler_params=pltpu.CompilerParams(vmem_limit_bytes=48 * 1024 * 1024),
    )(citations, doc_slot, doc_kv.reshape(docs_dev, dlen_local, rows, hdim))
    return out.reshape(ntraj * nhead, rows // nhead, dlen_local, hdim)


def attend_kernel(
    docs_dev, cites, group, scale,
    cit_ref, slot_ref, vis_ref, q_ref, do_ref, own_ref, arr_ref,
    o_ref, dq_ref, down_ref, part_ref,
    keys, vals, keys_t, vals_t, dkey, dval,
):
    seg = pl.program_id(1)
    me = lax.axis_index("dp")
    dlen = arr_ref.shape[1] * arr_ref.shape[3]
    hdim = q_ref.shape[-1]
    ndoc = cites * dlen
    total = keys.shape[0]
    tlen = total - ndoc

    def owner_of(c):
        return lax.div(slot_ref[cit_ref[me, c]], docs_dev)

    @pl.when(seg == 0)
    def _():
        for c in range(cites):
            owner = owner_of(c)
            keys[c * dlen : (c + 1) * dlen, :] = arr_ref[owner, :, 0].reshape(dlen, hdim)
            vals[c * dlen : (c + 1) * dlen, :] = arr_ref[owner, :, 1].reshape(dlen, hdim)
        keys[ndoc:, :] = own_ref[0, 0]
        vals[ndoc:, :] = own_ref[0, 1]
        keys_t[...] = keys[...].T
        vals_t[...] = vals[...].T
        dkey[...] = jnp.zeros_like(dkey)
        dval[...] = jnp.zeros_like(dval)

    q = q_ref[0]
    do = do_ref[0]
    lanes = q.shape[0]
    score = dot(keys[...], q, NT)
    pieces = []
    for c in range(cites):
        seen = vis_ref[0, c] <= seg
        pieces.append(jnp.where(seen, score[c * dlen : (c + 1) * dlen], -jnp.inf))
    key_pos = lax.broadcasted_iota(jnp.int32, (tlen, lanes), 0)
    token = seg * SEG + lax.broadcasted_iota(jnp.int32, (tlen, lanes), 1) // group
    pieces.append(jnp.where(key_pos <= token, score[ndoc:], -jnp.inf))
    score = jnp.concatenate(pieces, 0)
    top = jnp.max(score, axis=0, keepdims=True)
    weight = jnp.exp2((score - top) * (scale / math.log(2.0)))
    prob = weight * (1.0 / jnp.sum(weight, axis=0, keepdims=True))
    prob16 = prob.astype(BF16)
    out_t = dot(vals_t[...], prob16, NN).astype(BF16)
    o_ref[0] = out_t.T
    delta = jnp.sum(do.T.astype(F32) * out_t.astype(F32), axis=0, keepdims=True)
    dprob = dot(vals[...], do, NT)
    dscore = (prob * (dprob - delta)).astype(BF16)
    dq_ref[0] = (dot(keys_t[...], dscore, NN) * scale).astype(BF16).T
    dkey[...] += dot(dscore, q, NN)
    dval[...] += dot(prob16, do, NN)

    @pl.when(seg == pl.num_programs(1) - 1)
    def _():
        shape = part_ref.shape[1:2] + part_ref.shape[3:]
        for c in range(cites):
            owner = owner_of(c)
            rows = pl.ds(c * dlen, dlen)
            part_ref[owner, :, 0] = (dkey[rows, :] * scale).astype(BF16).reshape(shape)
            part_ref[owner, :, 1] = dval[rows, :].astype(BF16).reshape(shape)
        down_ref[0, 0] = (dkey[ndoc:, :] * scale).astype(BF16)
        down_ref[0, 1] = dval[ndoc:, :].astype(BF16)


def attend(citations, doc_slot, visible_from, q, do, own, arrived, docs_dev):
    kv_local, rows, hdim = q.shape
    tlen = own.shape[2]
    group = rows // tlen
    cites = citations.shape[1]
    ndp, nhead, _, dlen_local, _ = arrived.shape
    total = cites * dlen_local * nhead + tlen
    block = SEG * group
    row_spec = pl.BlockSpec((1, block, hdim), lambda g, s: (g, s, 0))
    own_spec = pl.BlockSpec((1, 2, tlen, hdim), lambda g, s: (g, 0, 0, 0))
    doc_spec = pl.BlockSpec((ndp, nhead, 2, dlen_local, hdim), lambda g, s: (0, 0, g, 0, 0))
    smem = pl.BlockSpec(memory_space=pltpu.SMEM)
    return pl.pallas_call(
        functools.partial(attend_kernel, docs_dev, cites, group, 1.0 / math.sqrt(hdim)),
        grid=(kv_local, rows // block),
        out_shape=(
            jax.ShapeDtypeStruct(q.shape, BF16),
            jax.ShapeDtypeStruct(q.shape, BF16),
            jax.ShapeDtypeStruct(own.shape, BF16),
            jax.ShapeDtypeStruct(arrived.shape, BF16),
        ),
        in_specs=[smem, smem, smem, row_spec, row_spec, own_spec, doc_spec],
        out_specs=(row_spec, row_spec, own_spec, doc_spec),
        scratch_shapes=[
            pltpu.VMEM((total, hdim), BF16),
            pltpu.VMEM((total, hdim), BF16),
            pltpu.VMEM((hdim, total), BF16),
            pltpu.VMEM((hdim, total), BF16),
            pltpu.VMEM((total, hdim), F32),
            pltpu.VMEM((total, hdim), F32),
        ],
        compiler_params=pltpu.CompilerParams(vmem_limit_bytes=56 * 1024 * 1024),
    )(citations, doc_slot, visible_from, q, do, own, arrived)


def settle_kernel(docs_dev, cites, cit_ref, slot_ref, got_ref, out_ref):
    me = lax.axis_index("dp")
    ntraj, nhead, per, _, _ = got_ref.shape
    out_ref[...] = jnp.zeros_like(out_ref)
    for t in range(ntraj):
        place = jnp.int32(-1)
        for c in range(cites):
            slot = slot_ref[cit_ref[t, c]]
            place = jnp.where(lax.div(slot, docs_dev) == me, lax.rem(slot, docs_dev), place)

        @pl.when(place >= 0)
        def _():
            for h in range(nhead):
                for r in range(per):
                    out_ref[place, :, h * per + r, :] += got_ref[t, h, r].astype(F32)


def settle(citations, doc_slot, got, docs_dev):
    ntraj, nhead, per, dlen_local, hdim = got.shape
    return pl.pallas_call(
        functools.partial(settle_kernel, docs_dev, citations.shape[1]),
        out_shape=jax.ShapeDtypeStruct((docs_dev, dlen_local, nhead * per, hdim), F32),
        in_specs=[
            pl.BlockSpec(memory_space=pltpu.SMEM),
            pl.BlockSpec(memory_space=pltpu.SMEM),
            pl.BlockSpec(memory_space=pltpu.VMEM),
        ],
        out_specs=pl.BlockSpec(memory_space=pltpu.VMEM),
        compiler_params=pltpu.CompilerParams(vmem_limit_bytes=48 * 1024 * 1024),
    )(citations, doc_slot, got)


def body(queries, traj_kv, grad_out, doc_kv, citations, doc_slot, visible_from):
    nhead = lax.axis_size("head")
    ndp = lax.axis_size("dp")
    tlen, heads_local, hdim = queries.shape
    kv_local = traj_kv.shape[1]
    group = heads_local // kv_local
    docs_dev, dlen_local = doc_kv.shape[:2]
    per = kv_local * 2
    outgoing = pack(citations, doc_slot, doc_kv, nhead)
    arrived = lax.all_to_all(outgoing, ("dp", "head"), split_axis=0, concat_axis=0, tiled=True)

    def by_kv(x):
        return x.reshape(tlen, kv_local, group, hdim).transpose(1, 0, 2, 3).reshape(kv_local, tlen * group, hdim)

    def by_token(x):
        return x.reshape(kv_local, tlen, group, hdim).transpose(1, 0, 2, 3).reshape(tlen, heads_local, hdim)

    attended, d_queries, d_own, part = attend(
        citations,
        doc_slot,
        visible_from,
        by_kv(queries),
        by_kv(grad_out),
        traj_kv.transpose(1, 2, 0, 3),
        arrived.reshape(ndp, nhead, per, dlen_local, hdim),
        docs_dev,
    )
    got = lax.all_to_all(
        part.reshape(outgoing.shape), ("dp", "head"), split_axis=0, concat_axis=0, tiled=True
    )
    d_doc = settle(citations, doc_slot, got.reshape(ndp, nhead, per, dlen_local, hdim), docs_dev)
    return (
        by_token(attended),
        by_token(d_queries),
        d_own.transpose(2, 0, 1, 3),
        d_doc.reshape(docs_dev, dlen_local, nhead * kv_local, 2, hdim),
    )


def solution(mesh):
    in_specs = (
        P("dp", "head", None),
        P("dp", "head", None, None),
        P("dp", "head", None),
        P("dp", "head", None, None, None),
        P(),
        P(),
        P("dp", None),
    )
    out_specs = (
        P("dp", "head", None),
        P("dp", "head", None),
        P("dp", "head", None, None),
        P("dp", "head", None, None, None),
    )
    return jax.shard_map(body, mesh=mesh, in_specs=in_specs, out_specs=out_specs, check_vma=False)
```

```python
import functools
import math

import jax
import jax.numpy as jnp
from jax import lax
from jax.experimental import pallas as pl
from jax.experimental.pallas import tpu as pltpu
from jax.sharding import PartitionSpec as P

SEG = 64
BF16 = jnp.bfloat16
F32 = jnp.float32
NT = (((1,), (1,)), ((), ()))
NN = (((1,), (0,)), ((), ()))


def dot(a, b, dims):
    return lax.dot_general(a, b, dims, preferred_element_type=F32)


def pack_kernel(docs_dev, cites, ntraj, cit_ref, slot_ref, doc_ref, out_ref, turned):
    me = lax.axis_index("dp")
    for d in range(docs_dev):
        turned[d] = jnp.swapaxes(doc_ref[d].astype(F32), 0, 1).astype(BF16)
    for t in range(ntraj):
        pick = jnp.int32(0)
        for c in range(cites):
            slot = slot_ref[cit_ref[t, c]]
            pick = jnp.where(lax.div(slot, docs_dev) == me, lax.rem(slot, docs_dev), pick)
        out_ref[t] = turned[pick]


def pack(citations, doc_slot, doc_kv, nhead):
    docs_dev, dlen_local, kv, two, hdim = doc_kv.shape
    ntraj, cites = citations.shape
    rows = kv * two
    out = pl.pallas_call(
        functools.partial(pack_kernel, docs_dev, cites, ntraj),
        out_shape=jax.ShapeDtypeStruct((ntraj, rows, dlen_local, hdim), BF16),
        in_specs=[
            pl.BlockSpec(memory_space=pltpu.SMEM),
            pl.BlockSpec(memory_space=pltpu.SMEM),
            pl.BlockSpec(memory_space=pltpu.VMEM),
        ],
        out_specs=pl.BlockSpec(memory_space=pltpu.VMEM),
        scratch_shapes=[pltpu.VMEM((docs_dev, rows, dlen_local, hdim), BF16)],
        compiler_params=pltpu.CompilerParams(vmem_limit_bytes=48 * 1024 * 1024),
    )(citations, doc_slot, doc_kv.reshape(docs_dev, dlen_local, rows, hdim))
    return out.reshape(ntraj * nhead, rows // nhead, dlen_local, hdim)


def own_kernel(group, rate, q_ref, do_ref, own_ref, stat_ref, part_ref, dot_ref, vals_t):
    seg = pl.program_id(0)
    kv_local, lanes, _ = q_ref.shape
    tlen = own_ref.shape[2]

    @pl.when(seg == 0)
    def _():
        for g in range(kv_local):
            vals_t[g] = own_ref[g, 1].T

    seen = own_seen(seg, tlen, lanes, group)
    for g in range(kv_local):
        score = jnp.where(seen, dot(own_ref[g, 0], q_ref[g], NT), -jnp.inf)
        top = jnp.max(score, axis=0, keepdims=True)
        weight = jnp.exp2((score - top) * rate)
        stat_ref[g, 0:1, :] = top
        stat_ref[g, 1:2, :] = jnp.sum(weight, axis=0, keepdims=True)
        part_ref[g] = dot(vals_t[g], weight.astype(BF16), NN)
        dot_ref[g] = do_ref[g].T


def own_seen(seg, tlen, lanes, group):
    key = lax.broadcasted_iota(jnp.int32, (tlen, lanes), 0)
    token = seg * SEG + lax.broadcasted_iota(jnp.int32, (tlen, lanes), 1) // group
    return key <= token


def docs_kernel(
    docs_dev, cites, rate, scale,
    cit_ref, slot_ref, vis_ref, q_ref, do_ref, dot_ref, stat_ref, own_ref, arr_ref,
    out_ref, final_ref, dscore_ref, part_ref,
    held, vals_t, weight, prob, dkey, dval, staged, sems,
):
    seg = pl.program_id(0)
    last = pl.num_programs(0) - 1
    me = lax.axis_index("dp")
    kv_local, lanes, hdim = q_ref.shape
    _, nhead, _, dlen_local, _ = held.shape
    dlen = nhead * dlen_local

    def owner_of(c):
        return lax.div(slot_ref[cit_ref[me, c]], docs_dev)

    def fetch(c):
        return pltpu.make_async_copy(arr_ref.at[owner_of(c)], held.at[c], sems.at[c])

    def give(c):
        return pltpu.make_async_copy(staged.at[c], part_ref.at[owner_of(c)], sems.at[c])

    def block(c, row):
        return held[c, :, row].reshape(dlen, hdim)

    @pl.when(seg == 0)
    def _():
        for c in range(cites):
            fetch(c).start()
        dkey[...] = jnp.zeros_like(dkey)
        dval[...] = jnp.zeros_like(dval)
        for c in range(cites):
            fetch(c).wait()
            for g in range(kv_local):
                vals_t[g, c] = block(c, 2 * g + 1).T

    for g in range(kv_local):
        q = q_ref[g]
        do = do_ref[g]
        own_top = stat_ref[g, 0:1, :]
        top = own_top
        tops = []
        sums = []
        for c in range(cites):
            score = dot(block(c, 2 * g), q, NT)
            doc_top = jnp.max(score, axis=0, keepdims=True)
            w = jnp.exp2((score - doc_top) * rate)
            weight[g, c] = w
            sums.append(jnp.sum(w, axis=0, keepdims=True))
            tops.append(jnp.where(vis_ref[0, c] <= seg, doc_top, -jnp.inf))
            top = jnp.maximum(top, tops[-1])
        own_factor = jnp.exp2((own_top - top) * rate)
        factors = [jnp.exp2((t - top) * rate) for t in tops]
        total = stat_ref[g, 1:2, :] * own_factor
        for f, s in zip(factors, sums):
            total = total + f * s
        inverse = 1.0 / total
        out = own_ref[g] * (own_factor * inverse)
        for c in range(cites):
            prob[g, c] = (weight[g, c] * (factors[c] * inverse)).astype(BF16)
            out = out + dot(vals_t[g, c], prob[g, c], NN)
        out = out.astype(BF16)
        out_ref[g] = out
        delta = jnp.sum(dot_ref[g].astype(F32) * out.astype(F32), axis=0, keepdims=True)
        final_ref[g, 0:1, :] = top
        final_ref[g, 1:2, :] = inverse
        final_ref[g, 2:3, :] = delta
        for c in range(cites):
            dprob = dot(block(c, 2 * g + 1), do, NT)
            p = prob[g, c]
            dscore = (p.astype(F32) * (dprob - delta)).astype(BF16)
            dscore_ref[g, c] = dscore
            dkey[g, c] += dot(dscore, q, NN)
            dval[g, c] += dot(p, do, NN)

    @pl.when(seg == last)
    def _():
        shape = (nhead, dlen_local, hdim)
        for c in range(cites):
            for g in range(kv_local):
                staged[c, :, 2 * g] = (dkey[g, c] * scale).astype(BF16).reshape(shape)
                staged[c, :, 2 * g + 1] = dval[g, c].astype(BF16).reshape(shape)
            give(c).start()
        for c in range(cites):
            give(c).wait()


def rest_kernel(
    docs_dev, cites, group, rate, scale,
    cit_ref, slot_ref, q_ref, do_ref, own_ref, arr_ref, out_ref, final_ref, dscore_ref,
    o_ref, dq_ref, down_ref,
    held, keys_t, own_t, dkey, dval, sems,
):
    seg = pl.program_id(0)
    last = pl.num_programs(0) - 1
    me = lax.axis_index("dp")
    kv_local, lanes, hdim = q_ref.shape
    _, nhead, _, dlen_local, _ = held.shape
    tlen = own_ref.shape[2]

    def fetch(c):
        owner = lax.div(slot_ref[cit_ref[me, c]], docs_dev)
        return pltpu.make_async_copy(arr_ref.at[owner], held.at[c], sems.at[c])

    @pl.when(seg == 0)
    def _():
        for c in range(cites):
            fetch(c).start()
        dkey[...] = jnp.zeros_like(dkey)
        dval[...] = jnp.zeros_like(dval)
        for g in range(kv_local):
            own_t[g] = own_ref[g, 0].T
        for c in range(cites):
            fetch(c).wait()
            for g in range(kv_local):
                keys_t[g, c] = held[c, :, 2 * g].reshape(nhead * dlen_local, hdim).T

    seen = own_seen(seg, tlen, lanes, group)
    for g in range(kv_local):
        q = q_ref[g]
        do = do_ref[g]
        top = final_ref[g, 0:1, :]
        inverse = final_ref[g, 1:2, :]
        delta = final_ref[g, 2:3, :]
        score = jnp.where(seen, dot(own_ref[g, 0], q, NT), -jnp.inf)
        prob = jnp.exp2((score - top) * rate) * inverse
        dprob = dot(own_ref[g, 1], do, NT)
        dscore = (prob * (dprob - delta)).astype(BF16)
        dkey[g] += dot(dscore, q, NN)
        dval[g] += dot(prob.astype(BF16), do, NN)
        dq = dot(own_t[g], dscore, NN)
        for c in range(cites):
            dq = dq + dot(keys_t[g, c], dscore_ref[g, c], NN)
        dq_ref[g] = (dq * scale).astype(BF16).T
        o_ref[g] = out_ref[g].T

    @pl.when(seg == last)
    def _():
        down_ref[:, 0] = (dkey[...] * scale).astype(BF16)
        down_ref[:, 1] = dval[...].astype(BF16)


SMEM = pl.BlockSpec(memory_space=pltpu.SMEM)
ANY = pl.BlockSpec(memory_space=pl.ANY)


def params(megabytes):
    return pltpu.CompilerParams(vmem_limit_bytes=megabytes * 1024 * 1024)


def cost(*shape):
    flops = 2 * math.prod(shape)
    return pl.CostEstimate(flops=flops, bytes_accessed=8 * 1024 * 1024, transcendentals=0)


def attend_own(q, do, own):
    kv_local, rows, hdim = q.shape
    tlen = own.shape[2]
    group = rows // tlen
    block = SEG * group
    row_spec = pl.BlockSpec((kv_local, block, hdim), lambda s: (0, s, 0))
    lane_spec = pl.BlockSpec((kv_local, hdim, block), lambda s: (0, 0, s))
    stat_spec = pl.BlockSpec((kv_local, 8, block), lambda s: (0, 0, s))
    whole_own = pl.BlockSpec(own.shape, lambda s: (0, 0, 0, 0))
    return pl.pallas_call(
        functools.partial(own_kernel, group, 1.0 / (math.sqrt(hdim) * math.log(2.0))),
        grid=(rows // block,),
        out_shape=(
            jax.ShapeDtypeStruct((kv_local, 8, rows), F32),
            jax.ShapeDtypeStruct((kv_local, hdim, rows), F32),
            jax.ShapeDtypeStruct((kv_local, hdim, rows), BF16),
        ),
        in_specs=[row_spec, row_spec, whole_own],
        out_specs=(stat_spec, lane_spec, lane_spec),
        scratch_shapes=[pltpu.VMEM((kv_local, hdim, tlen), BF16)],
        compiler_params=params(40),
        cost_estimate=cost(kv_local, rows, tlen, hdim, 2),
    )(q, do, own)


def attend_docs(
    citations, doc_slot, visible_from, q, do, do_t, stat, own_part, arrived, docs_dev, group
):
    kv_local, rows, hdim = q.shape
    cites = citations.shape[1]
    _, nhead, per, dlen_local, _ = arrived.shape
    dlen = nhead * dlen_local
    block = SEG * group
    nseg = rows // block
    row_spec = pl.BlockSpec((kv_local, block, hdim), lambda s: (0, s, 0))
    lane_spec = pl.BlockSpec((kv_local, hdim, block), lambda s: (0, 0, s))
    stat_spec = pl.BlockSpec((kv_local, 8, block), lambda s: (0, 0, s))
    score_spec = pl.BlockSpec((kv_local, cites, dlen, block), lambda s: (0, 0, 0, s))
    rate = 1.0 / (math.sqrt(hdim) * math.log(2.0))
    return pl.pallas_call(
        functools.partial(docs_kernel, docs_dev, cites, rate, 1.0 / math.sqrt(hdim)),
        grid=(nseg,),
        out_shape=(
            jax.ShapeDtypeStruct((kv_local, hdim, rows), BF16),
            jax.ShapeDtypeStruct((kv_local, 8, rows), F32),
            jax.ShapeDtypeStruct((kv_local, cites, dlen, rows), BF16),
            jax.ShapeDtypeStruct(arrived.shape, BF16),
        ),
        in_specs=[SMEM, SMEM, SMEM, row_spec, row_spec, lane_spec, stat_spec, lane_spec, ANY],
        out_specs=(lane_spec, stat_spec, score_spec, ANY),
        scratch_shapes=[
            pltpu.VMEM((cites, nhead, per, dlen_local, hdim), BF16),
            pltpu.VMEM((kv_local, cites, hdim, dlen), BF16),
            pltpu.VMEM((kv_local, cites, dlen, block), F32),
            pltpu.VMEM((kv_local, cites, dlen, block), BF16),
            pltpu.VMEM((kv_local, cites, dlen, hdim), F32),
            pltpu.VMEM((kv_local, cites, dlen, hdim), F32),
            pltpu.VMEM((cites, nhead, per, dlen_local, hdim), BF16),
            pltpu.SemaphoreType.DMA((cites,)),
        ],
        compiler_params=params(56),
        cost_estimate=cost(kv_local, rows, cites * dlen, hdim, 5),
    )(citations, doc_slot, visible_from, q, do, do_t, stat, own_part, arrived)


def attend_rest(citations, doc_slot, q, do, own, arrived, out_t, final, dscore, docs_dev):
    kv_local, rows, hdim = q.shape
    tlen = own.shape[2]
    group = rows // tlen
    cites = citations.shape[1]
    _, nhead, per, dlen_local, _ = arrived.shape
    dlen = nhead * dlen_local
    block = SEG * group
    row_spec = pl.BlockSpec((kv_local, block, hdim), lambda s: (0, s, 0))
    lane_spec = pl.BlockSpec((kv_local, hdim, block), lambda s: (0, 0, s))
    stat_spec = pl.BlockSpec((kv_local, 8, block), lambda s: (0, 0, s))
    score_spec = pl.BlockSpec((kv_local, cites, dlen, block), lambda s: (0, 0, 0, s))
    whole_own = pl.BlockSpec(own.shape, lambda s: (0, 0, 0, 0))
    rate = 1.0 / (math.sqrt(hdim) * math.log(2.0))
    return pl.pallas_call(
        functools.partial(rest_kernel, docs_dev, cites, group, rate, 1.0 / math.sqrt(hdim)),
        grid=(rows // block,),
        out_shape=(
            jax.ShapeDtypeStruct(q.shape, BF16),
            jax.ShapeDtypeStruct(q.shape, BF16),
            jax.ShapeDtypeStruct(own.shape, BF16),
        ),
        in_specs=[SMEM, SMEM, row_spec, row_spec, whole_own, ANY, lane_spec, stat_spec, score_spec],
        out_specs=(row_spec, row_spec, whole_own),
        scratch_shapes=[
            pltpu.VMEM((cites, nhead, per, dlen_local, hdim), BF16),
            pltpu.VMEM((kv_local, cites, hdim, dlen), BF16),
            pltpu.VMEM((kv_local, hdim, tlen), BF16),
            pltpu.VMEM((kv_local, tlen, hdim), F32),
            pltpu.VMEM((kv_local, tlen, hdim), F32),
            pltpu.SemaphoreType.DMA((cites,)),
        ],
        compiler_params=params(48),
        cost_estimate=cost(kv_local, rows, cites * dlen + 5 * tlen, hdim),
    )(citations, doc_slot, q, do, own, arrived, out_t, final, dscore)


def settle_kernel(docs_dev, cites, cit_ref, slot_ref, got_ref, out_ref):
    me = lax.axis_index("dp")
    ntraj, nhead, per, _, _ = got_ref.shape
    out_ref[...] = jnp.zeros_like(out_ref)
    for t in range(ntraj):
        place = jnp.int32(-1)
        for c in range(cites):
            slot = slot_ref[cit_ref[t, c]]
            place = jnp.where(lax.div(slot, docs_dev) == me, lax.rem(slot, docs_dev), place)

        @pl.when(place >= 0)
        def _():
            for h in range(nhead):
                for r in range(per):
                    out_ref[place, :, h * per + r, :] += got_ref[t, h, r].astype(F32)


def settle(citations, doc_slot, got, docs_dev):
    ntraj, nhead, per, dlen_local, hdim = got.shape
    return pl.pallas_call(
        functools.partial(settle_kernel, docs_dev, citations.shape[1]),
        out_shape=jax.ShapeDtypeStruct((docs_dev, dlen_local, nhead * per, hdim), F32),
        in_specs=[
            pl.BlockSpec(memory_space=pltpu.SMEM),
            pl.BlockSpec(memory_space=pltpu.SMEM),
            pl.BlockSpec(memory_space=pltpu.VMEM),
        ],
        out_specs=pl.BlockSpec(memory_space=pltpu.VMEM),
        compiler_params=pltpu.CompilerParams(vmem_limit_bytes=48 * 1024 * 1024),
    )(citations, doc_slot, got)


def body(queries, traj_kv, grad_out, doc_kv, citations, doc_slot, visible_from):
    nhead = lax.axis_size("head")
    ndp = lax.axis_size("dp")
    tlen, heads_local, hdim = queries.shape
    kv_local = traj_kv.shape[1]
    group = heads_local // kv_local
    docs_dev, dlen_local = doc_kv.shape[:2]
    per = kv_local * 2
    outgoing = pack(citations, doc_slot, doc_kv, nhead)
    arrived = lax.all_to_all(outgoing, ("dp", "head"), split_axis=0, concat_axis=0, tiled=True)

    def by_kv(x):
        return x.reshape(tlen, kv_local, group, hdim).transpose(1, 0, 2, 3).reshape(kv_local, tlen * group, hdim)

    def by_token(x):
        return x.reshape(kv_local, tlen, group, hdim).transpose(1, 0, 2, 3).reshape(tlen, heads_local, hdim)

    q = by_kv(queries)
    do = by_kv(grad_out)
    own = traj_kv.transpose(1, 2, 0, 3)
    stat, own_part, do_t = attend_own(q, do, own)
    arrived = arrived.reshape(ndp, nhead, per, dlen_local, hdim)
    out_t, final, dscore, part = attend_docs(
        citations, doc_slot, visible_from, q, do, do_t, stat, own_part, arrived, docs_dev, group
    )
    got = lax.all_to_all(
        part.reshape(outgoing.shape), ("dp", "head"), split_axis=0, concat_axis=0, tiled=True
    )
    attended, d_queries, d_own = attend_rest(
        citations, doc_slot, q, do, own, arrived, out_t, final, dscore, docs_dev
    )
    d_doc = settle(citations, doc_slot, got.reshape(ndp, nhead, per, dlen_local, hdim), docs_dev)
    return (
        by_token(attended),
        by_token(d_queries),
        d_own.transpose(2, 0, 1, 3),
        d_doc.reshape(docs_dev, dlen_local, nhead * kv_local, 2, hdim),
    )


def solution(mesh):
    in_specs = (
        P("dp", "head", None),
        P("dp", "head", None, None),
        P("dp", "head", None),
        P("dp", "head", None, None, None),
        P(),
        P(),
        P("dp", None),
    )
    out_specs = (
        P("dp", "head", None),
        P("dp", "head", None),
        P("dp", "head", None, None),
        P("dp", "head", None, None, None),
    )
    return jax.shard_map(body, mesh=mesh, in_specs=in_specs, out_specs=out_specs, check_vma=False)
```

```python
import functools
import math

import jax
import jax.numpy as jnp
from jax import lax
from jax.experimental import pallas as pl
from jax.experimental.pallas import tpu as pltpu
from jax.sharding import PartitionSpec as P

SEG = 64
BF16 = jnp.bfloat16
F32 = jnp.float32
NT = (((1,), (1,)), ((), ()))
NN = (((1,), (0,)), ((), ()))
SMEM = pl.BlockSpec(memory_space=pltpu.SMEM)
VMEM = pl.BlockSpec(memory_space=pltpu.VMEM)
ANY = pl.BlockSpec(memory_space=pl.ANY)


def dot(a, b, dims):
    return lax.dot_general(a, b, dims, preferred_element_type=F32)


def params(megabytes):
    return pltpu.CompilerParams(vmem_limit_bytes=megabytes * 1024 * 1024)


def cost(*shape):
    flops = 2 * math.prod(shape)
    return pl.CostEstimate(flops=flops, bytes_accessed=8 * 1024 * 1024, transcendentals=0)


def place_of(cit_ref, slot_ref, t, cites, docs_dev, me):
    place = jnp.int32(-1)
    for c in range(cites):
        slot = slot_ref[cit_ref[c, t]]
        place = jnp.where(lax.div(slot, docs_dev) == me, lax.rem(slot, docs_dev), place)
    return place


def pack_kernel(cit_ref, slot_ref, doc_ref, out_ref, held, turned, in_sems, out_sems):
    me = lax.axis_index("dp")
    cites, ntraj = cit_ref.shape
    docs_dev = doc_ref.shape[0]
    loads = [pltpu.make_async_copy(doc_ref.at[d], held.at[d], in_sems.at[d]) for d in range(docs_dev)]
    for load in loads:
        load.start()
    places = [place_of(cit_ref, slot_ref, t, cites, docs_dev, me) for t in range(ntraj)]
    for d in range(docs_dev):
        loads[d].wait()
        turned[d] = jnp.swapaxes(held[d].astype(F32), 0, 1).astype(BF16)
    stores = []
    for t in range(ntraj):
        source = turned.at[jnp.maximum(places[t], 0)]
        stores.append(pltpu.make_async_copy(source, out_ref.at[t], out_sems.at[t]))
        stores[-1].start()
    for store in stores:
        store.wait()


def pack(cit, doc_slot, doc_kv, nhead):
    docs_dev, dlen_local, kv, two, hdim = doc_kv.shape
    ntraj = cit.shape[1]
    rows = kv * two
    out = pl.pallas_call(
        pack_kernel,
        out_shape=jax.ShapeDtypeStruct((ntraj, rows, dlen_local, hdim), BF16),
        in_specs=[SMEM, SMEM, ANY],
        out_specs=ANY,
        scratch_shapes=[
            pltpu.VMEM((docs_dev, dlen_local, rows, hdim), BF16),
            pltpu.VMEM((docs_dev, rows, dlen_local, hdim), BF16),
            pltpu.SemaphoreType.DMA((docs_dev,)),
            pltpu.SemaphoreType.DMA((ntraj,)),
        ],
        compiler_params=params(60),
    )(cit, doc_slot, doc_kv.reshape(docs_dev, dlen_local, rows, hdim))
    return out.reshape(ntraj * nhead, rows // nhead, dlen_local, hdim)


def own_seen(seg, tlen, lanes, group):
    key = lax.broadcasted_iota(jnp.int32, (tlen, lanes), 0)
    token = seg * SEG + lax.broadcasted_iota(jnp.int32, (tlen, lanes), 1) // group
    return key <= token


def own_kernel(group, rate, q_ref, own_ref, stat_ref, part_ref, vals_t):
    seg = pl.program_id(0)
    kv_local, _, lanes, _ = q_ref.shape
    tlen = own_ref.shape[2]

    @pl.when(seg == 0)
    def _():
        for g in range(kv_local):
            vals_t[g] = own_ref[g, 1].T

    seen = own_seen(seg, tlen, lanes, group)
    for g in range(kv_local):
        score = jnp.where(seen, dot(own_ref[g, 0], q_ref[g, 0], NT), -jnp.inf)
        top = jnp.max(score, axis=0, keepdims=True)
        weight = jnp.exp2((score - top) * rate)
        stat_ref[g, 0, 0:1, :] = top
        stat_ref[g, 0, 1:2, :] = jnp.sum(weight, axis=0, keepdims=True)
        part_ref[g, 0] = dot(vals_t[g], weight.astype(BF16), NN)


def seg_spec(kv_local, rows, columns):
    return pl.BlockSpec((kv_local, 1, rows, columns), lambda s: (0, s, 0, 0))


def attend_own(q, own):
    kv_local, nseg, block, hdim = q.shape
    tlen = own.shape[2]
    return pl.pallas_call(
        functools.partial(own_kernel, block // SEG, 1.0 / (math.sqrt(hdim) * math.log(2.0))),
        grid=(nseg,),
        out_shape=(
            jax.ShapeDtypeStruct((kv_local, nseg, 8, block), F32),
            jax.ShapeDtypeStruct((kv_local, nseg, hdim, block), F32),
        ),
        in_specs=[
            seg_spec(kv_local, block, hdim),
            pl.BlockSpec(own.shape, lambda s: (0, 0, 0, 0)),
        ],
        out_specs=(seg_spec(kv_local, 8, block), seg_spec(kv_local, hdim, block)),
        scratch_shapes=[pltpu.VMEM((kv_local, hdim, tlen), BF16)],
        compiler_params=params(32),
        cost_estimate=cost(kv_local, nseg, block, tlen, hdim, 2),
    )(q, own)


def docs_kernel(
    docs_dev, rate, scale, depth,
    cit_ref, slot_ref, vis_ref, q_ref, do_ref, stat_ref, own_ref, arr_ref,
    out_ref, final_ref, part_ref,
    keys, vals, vals_t, dkey, dval,
):
    me = lax.axis_index("dp")
    cites = cit_ref.shape[0]
    kv_local, nseg, _, hdim = q_ref.shape
    _, nhead, _, dlen_local, _ = arr_ref.shape
    dlen = nhead * dlen_local
    owners = [lax.div(slot_ref[cit_ref[c, me]], docs_dev) for c in range(cites)]
    for c in range(cites):
        rows = pl.ds(c * dlen, dlen)
        for g in range(kv_local):
            keys[g, rows, :] = arr_ref[owners[c], :, 2 * g].reshape(dlen, hdim)
            value = arr_ref[owners[c], :, 2 * g + 1].reshape(dlen, hdim)
            vals[g, rows, :] = value
            vals_t[g, :, rows] = value.T

    def add(ref, g, seg, term):
        ref[g] = term if seg == 0 else ref[g] + term

    def stages(g, seg):
        q = q_ref[g, seg]
        do = do_ref[g, seg]
        score = dot(keys[g], q, NT)
        yield
        own_top = stat_ref[g, seg, 0:1, :]
        top = own_top
        tops = []
        sums = []
        weights = []
        for c in range(cites):
            part = score[c * dlen : (c + 1) * dlen]
            doc_top = jnp.max(part, axis=0, keepdims=True)
            weights.append(jnp.exp2((part - doc_top) * rate))
            sums.append(jnp.sum(weights[-1], axis=0, keepdims=True))
            tops.append(jnp.where(vis_ref[0, c] <= seg, doc_top, -jnp.inf))
            top = jnp.maximum(top, tops[-1])
        own_factor = jnp.exp2((own_top - top) * rate)
        factors = [jnp.exp2((t - top) * rate) for t in tops]
        total = stat_ref[g, seg, 1:2, :] * own_factor
        for f, s in zip(factors, sums):
            total = total + f * s
        inverse = 1.0 / total
        prob = jnp.concatenate([(w * (f * inverse)).astype(BF16) for w, f in zip(weights, factors)], 0)
        yield
        out = own_ref[g, seg] * (own_factor * inverse) + dot(vals_t[g], prob, NN)
        add(dval, g, seg, dot(prob, do, NN))
        out = out.astype(BF16)
        out_ref[g, seg] = out
        yield
        delta = jnp.sum(do.T.astype(F32) * out.astype(F32), axis=0, keepdims=True)
        final_ref[g, seg, 0:1, :] = top
        final_ref[g, seg, 1:2, :] = inverse
        final_ref[g, seg, 2:3, :] = delta
        dprob = dot(vals[g], do, NT)
        dscore = (prob.astype(F32) * (dprob - delta)).astype(BF16)
        yield
        add(dkey, g, seg, dot(dscore, q, NN))

    waiting = [stages(g, seg) for seg in range(nseg) for g in range(kv_local)]
    active = []
    while waiting or active:
        if waiting and len(active) < depth:
            active.append(waiting.pop(0))
        active = [item for item in active if next(item, "end") != "end"]

    shape = (nhead, dlen_local, hdim)
    for c in range(cites):
        rows = pl.ds(c * dlen, dlen)
        for g in range(kv_local):
            part_ref[owners[c], :, 2 * g] = (dkey[g, rows, :] * scale).astype(BF16).reshape(shape)
            part_ref[owners[c], :, 2 * g + 1] = dval[g, rows, :].astype(BF16).reshape(shape)


def attend_docs(cit, doc_slot, visible_from, q, do, stat, own_part, arrived, docs_dev):
    kv_local, nseg, block, hdim = q.shape
    cites = cit.shape[0]
    _, nhead, per, dlen_local, _ = arrived.shape
    ndoc = cites * nhead * dlen_local
    rate = 1.0 / (math.sqrt(hdim) * math.log(2.0))
    depth = 5 if ndoc <= 512 else 1

    def near(x):
        return pltpu.with_memory_space_constraint(x, pltpu.VMEM)

    return pl.pallas_call(
        functools.partial(docs_kernel, docs_dev, rate, 1.0 / math.sqrt(hdim), depth),
        out_shape=(
            jax.ShapeDtypeStruct((kv_local, nseg, hdim, block), BF16),
            jax.ShapeDtypeStruct((kv_local, nseg, 8, block), F32),
            jax.ShapeDtypeStruct(arrived.shape, BF16),
        ),
        in_specs=[SMEM, SMEM, SMEM, VMEM, VMEM, VMEM, VMEM, VMEM],
        out_specs=(VMEM, VMEM, VMEM),
        scratch_shapes=[
            pltpu.VMEM((kv_local, ndoc, hdim), BF16),
            pltpu.VMEM((kv_local, ndoc, hdim), BF16),
            pltpu.VMEM((kv_local, hdim, ndoc), BF16),
            pltpu.VMEM((kv_local, ndoc, hdim), F32),
            pltpu.VMEM((kv_local, ndoc, hdim), F32),
        ],
        compiler_params=params(40),
        cost_estimate=cost(kv_local, nseg, block, ndoc, hdim, 5),
    )(cit, doc_slot, visible_from, near(q), near(do), near(stat), near(own_part), near(arrived))


def rest_kernel(
    docs_dev, group, rate, scale,
    cit_ref, slot_ref, vis_ref, q_ref, do_ref, own_ref, arr_ref, out_ref, final_ref,
    o_ref, dq_ref, down_ref,
    held, keys, vals, keys_t, dkey, dval, sems,
):
    seg = pl.program_id(0)
    last = pl.num_programs(0) - 1
    me = lax.axis_index("dp")
    kv_local, _, lanes, hdim = q_ref.shape
    cites, nhead, _, dlen_local, _ = held.shape
    dlen = nhead * dlen_local
    ndoc = cites * dlen
    tlen = own_ref.shape[2]

    def fetch(c):
        owner = lax.div(slot_ref[cit_ref[c, me]], docs_dev)
        return pltpu.make_async_copy(arr_ref.at[owner], held.at[c], sems.at[c])

    @pl.when(seg == 0)
    def _():
        for c in range(cites):
            fetch(c).start()
        dkey[...] = jnp.zeros_like(dkey)
        dval[...] = jnp.zeros_like(dval)
        for g in range(kv_local):
            keys[g, ndoc:, :] = own_ref[g, 0]
            vals[g, ndoc:, :] = own_ref[g, 1]
        for c in range(cites):
            fetch(c).wait()
            rows = pl.ds(c * dlen, dlen)
            for g in range(kv_local):
                keys[g, rows, :] = held[c, :, 2 * g].reshape(dlen, hdim)
                vals[g, rows, :] = held[c, :, 2 * g + 1].reshape(dlen, hdim)
        for g in range(kv_local):
            keys_t[g] = keys[g].T

    seen = own_seen(seg, tlen, lanes, group)
    for g in range(kv_local):
        q = q_ref[g, 0]
        do = do_ref[g, 0]
        top = final_ref[g, 0, 0:1, :]
        inverse = final_ref[g, 0, 1:2, :]
        delta = final_ref[g, 0, 2:3, :]
        score = dot(keys[g], q, NT)
        parts = [
            jnp.where(vis_ref[0, c] <= seg, score[c * dlen : (c + 1) * dlen], -jnp.inf)
            for c in range(cites)
        ]
        parts.append(jnp.where(seen, score[ndoc:], -jnp.inf))
        prob = jnp.exp2((jnp.concatenate(parts, 0) - top) * rate) * inverse
        dprob = dot(vals[g], do, NT)
        dscore = (prob * (dprob - delta)).astype(BF16)
        dkey[g] += dot(dscore[ndoc:], q, NN)
        dval[g] += dot(prob[ndoc:].astype(BF16), do, NN)
        dq_ref[g, 0] = (dot(keys_t[g], dscore, NN) * scale).astype(BF16).T
        o_ref[g, 0] = out_ref[g, 0].T

    @pl.when(seg == last)
    def _():
        down_ref[:, 0] = (dkey[...] * scale).astype(BF16)
        down_ref[:, 1] = dval[...].astype(BF16)


def attend_rest(cit, doc_slot, visible_from, q, do, own, arrived, out_t, final, docs_dev):
    kv_local, nseg, block, hdim = q.shape
    tlen = own.shape[2]
    cites = cit.shape[0]
    _, nhead, per, dlen_local, _ = arrived.shape
    total = cites * nhead * dlen_local + tlen
    row_spec = seg_spec(kv_local, block, hdim)
    whole_own = pl.BlockSpec(own.shape, lambda s: (0, 0, 0, 0))
    rate = 1.0 / (math.sqrt(hdim) * math.log(2.0))
    return pl.pallas_call(
        functools.partial(rest_kernel, docs_dev, block // SEG, rate, 1.0 / math.sqrt(hdim)),
        grid=(nseg,),
        out_shape=(
            jax.ShapeDtypeStruct(q.shape, BF16),
            jax.ShapeDtypeStruct(q.shape, BF16),
            jax.ShapeDtypeStruct(own.shape, BF16),
        ),
        in_specs=[
            SMEM, SMEM, SMEM, row_spec, row_spec, whole_own, ANY,
            seg_spec(kv_local, hdim, block), seg_spec(kv_local, 8, block),
        ],
        out_specs=(row_spec, row_spec, whole_own),
        scratch_shapes=[
            pltpu.VMEM((cites, nhead, per, dlen_local, hdim), BF16),
            pltpu.VMEM((kv_local, total, hdim), BF16),
            pltpu.VMEM((kv_local, total, hdim), BF16),
            pltpu.VMEM((kv_local, hdim, total), BF16),
            pltpu.VMEM((kv_local, tlen, hdim), F32),
            pltpu.VMEM((kv_local, tlen, hdim), F32),
            pltpu.SemaphoreType.DMA((cites,)),
        ],
        compiler_params=params(40),
        cost_estimate=cost(kv_local, nseg, block, 3 * total, hdim),
    )(cit, doc_slot, visible_from, q, do, own, arrived, out_t, final)


def settle_kernel(cit_ref, slot_ref, got_ref, out_ref, total, turned, sems):
    me = lax.axis_index("dp")
    ntraj, nhead, per, dlen_local, hdim = got_ref.shape
    cites = cit_ref.shape[0]
    docs_dev = out_ref.shape[0]
    places = [place_of(cit_ref, slot_ref, t, cites, docs_dev, me) for t in range(ntraj)]
    stores = []
    for d in range(docs_dev):
        total[d] = jnp.zeros_like(total[d])
        for t in range(ntraj):

            @pl.when(places[t] == d)
            def _():
                total[d] += got_ref[t].astype(F32)

        turned[d] = jnp.swapaxes(total[d].reshape(nhead * per, dlen_local, hdim), 0, 1)
        stores.append(pltpu.make_async_copy(turned.at[d], out_ref.at[d], sems.at[d]))
        stores[-1].start()
    for store in stores:
        store.wait()


def settle(cit, doc_slot, got, docs_dev):
    _, nhead, per, dlen_local, hdim = got.shape
    return pl.pallas_call(
        settle_kernel,
        out_shape=jax.ShapeDtypeStruct((docs_dev, dlen_local, nhead * per, hdim), F32),
        in_specs=[SMEM, SMEM, VMEM],
        out_specs=ANY,
        scratch_shapes=[
            pltpu.VMEM((docs_dev, nhead, per, dlen_local, hdim), F32),
            pltpu.VMEM((docs_dev, dlen_local, nhead * per, hdim), F32),
            pltpu.SemaphoreType.DMA((docs_dev,)),
        ],
        compiler_params=params(32),
    )(cit, doc_slot, pltpu.with_memory_space_constraint(got, pltpu.VMEM))


def body(queries, traj_kv, grad_out, doc_kv, citations, doc_slot, visible_from):
    nhead = lax.axis_size("head")
    ndp = lax.axis_size("dp")
    tlen, heads_local, hdim = queries.shape
    kv_local = traj_kv.shape[1]
    group = heads_local // kv_local
    docs_dev, dlen_local = doc_kv.shape[:2]
    per = kv_local * 2
    cit = citations.T
    outgoing = pack(cit, doc_slot, doc_kv, nhead)
    arrived = lax.all_to_all(outgoing, ("dp", "head"), split_axis=0, concat_axis=0, tiled=True)
    arrived = arrived.reshape(ndp, nhead, per, dlen_local, hdim)

    def by_kv(x):
        x = x.reshape(tlen, kv_local, group, hdim).transpose(1, 0, 2, 3)
        return x.reshape(kv_local, tlen // SEG, SEG * group, hdim)

    def by_token(x):
        x = x.reshape(kv_local, tlen, group, hdim).transpose(1, 0, 2, 3)
        return x.reshape(tlen, heads_local, hdim)

    q = by_kv(queries)
    do = by_kv(grad_out)
    own = traj_kv.transpose(1, 2, 0, 3)
    stat, own_part = attend_own(q, own)
    out_t, final, part = attend_docs(
        cit, doc_slot, visible_from, q, do, stat, own_part, arrived, docs_dev
    )
    got = lax.all_to_all(
        part.reshape(outgoing.shape), ("dp", "head"), split_axis=0, concat_axis=0, tiled=True
    )
    attended, d_queries, d_own = attend_rest(
        cit, doc_slot, visible_from, q, do, own, arrived, out_t, final, docs_dev
    )
    d_doc = settle(cit, doc_slot, got.reshape(ndp, nhead, per, dlen_local, hdim), docs_dev)
    return (
        by_token(attended),
        by_token(d_queries),
        d_own.transpose(2, 0, 1, 3),
        d_doc.reshape(docs_dev, dlen_local, nhead * kv_local, 2, hdim),
    )


def solution(mesh):
    in_specs = (
        P("dp", "head", None),
        P("dp", "head", None, None),
        P("dp", "head", None),
        P("dp", "head", None, None, None),
        P(),
        P(),
        P("dp", None),
    )
    out_specs = (
        P("dp", "head", None),
        P("dp", "head", None),
        P("dp", "head", None, None),
        P("dp", "head", None, None, None),
    )
    return jax.shard_map(body, mesh=mesh, in_specs=in_specs, out_specs=out_specs, check_vma=False)
```

```python
import functools
import math

import jax
import jax.numpy as jnp
from jax import lax
from jax.experimental import pallas as pl
from jax.experimental.pallas import tpu as pltpu
from jax.sharding import PartitionSpec as P

SEG = 64
BF16 = jnp.bfloat16
F32 = jnp.float32
NT = (((1,), (1,)), ((), ()))
NN = (((1,), (0,)), ((), ()))
SMEM = pl.BlockSpec(memory_space=pltpu.SMEM)
VMEM = pl.BlockSpec(memory_space=pltpu.VMEM)
HBM = pl.BlockSpec(memory_space=pltpu.HBM)


def dot(a, b, dims):
    return lax.dot_general(a, b, dims, preferred_element_type=F32)


def params(megabytes):
    return pltpu.CompilerParams(vmem_limit_bytes=megabytes * 1024 * 1024)


def cost(*shape):
    flops = 2 * math.prod(shape)
    return pl.CostEstimate(flops=flops, bytes_accessed=8 * 1024 * 1024, transcendentals=0)


def near(x):
    return pltpu.with_memory_space_constraint(x, pltpu.VMEM)


def scalar(x):
    return pltpu.with_memory_space_constraint(x, pltpu.SMEM)


def place_of(cit_ref, slot_ref, t, cites, docs_dev, me):
    place = jnp.int32(-1)
    for c in range(cites):
        slot = slot_ref[cit_ref[c, t]]
        place = jnp.where(lax.div(slot, docs_dev) == me, lax.rem(slot, docs_dev), place)
    return place


def pack_kernel(cit_hbm, slot_hbm, doc_ref, out_ref, cit_ref, slot_ref, held, turned, in_sems, out_sems):
    me = lax.axis_index("dp")
    cites, ntraj = cit_ref.shape
    docs_dev = doc_ref.shape[0]
    scalars = [
        pltpu.make_async_copy(cit_hbm, cit_ref, in_sems.at[docs_dev]),
        pltpu.make_async_copy(slot_hbm, slot_ref, in_sems.at[docs_dev + 1]),
    ]
    for load in scalars:
        load.start()
    loads = [pltpu.make_async_copy(doc_ref.at[d], held.at[d], in_sems.at[d]) for d in range(docs_dev)]
    for load in loads:
        load.start()
    for load in scalars:
        load.wait()
    places = [place_of(cit_ref, slot_ref, t, cites, docs_dev, me) for t in range(ntraj)]
    for d in range(docs_dev):
        loads[d].wait()
        turned[d] = jnp.swapaxes(held[d].astype(F32), 0, 1).astype(BF16)
    stores = []
    for t in range(ntraj):
        source = turned.at[jnp.maximum(places[t], 0)]
        stores.append(pltpu.make_async_copy(source, out_ref.at[t], out_sems.at[t]))
        stores[-1].start()
    for store in stores:
        store.wait()


def pack(cit, doc_slot, doc_kv, nhead):
    docs_dev, dlen_local, kv, two, hdim = doc_kv.shape
    ntraj = cit.shape[1]
    rows = kv * two
    out = pl.pallas_call(
        pack_kernel,
        out_shape=jax.ShapeDtypeStruct((ntraj, rows, dlen_local, hdim), BF16),
        in_specs=[HBM, HBM, HBM],
        out_specs=HBM,
        scratch_shapes=[
            pltpu.SMEM(cit.shape, jnp.int32),
            pltpu.SMEM(doc_slot.shape, jnp.int32),
            pltpu.VMEM((docs_dev, dlen_local, rows, hdim), BF16),
            pltpu.VMEM((docs_dev, rows, dlen_local, hdim), BF16),
            pltpu.SemaphoreType.DMA((docs_dev + 2,)),
            pltpu.SemaphoreType.DMA((ntraj,)),
        ],
        compiler_params=params(60),
    )(cit, doc_slot, doc_kv.reshape(docs_dev, dlen_local, rows, hdim))
    return out.reshape(ntraj * nhead, rows // nhead, dlen_local, hdim)


def own_seen(seg, tlen, lanes, group):
    key = lax.broadcasted_iota(jnp.int32, (tlen, lanes), 0)
    token = seg * SEG + lax.broadcasted_iota(jnp.int32, (tlen, lanes), 1) // group
    return key <= token


def own_kernel(group, rate, q_ref, own_ref, stat_ref, part_ref, vals_t):
    seg = pl.program_id(0)
    kv_local, _, lanes, _ = q_ref.shape
    tlen = own_ref.shape[2]

    @pl.when(seg == 0)
    def _():
        for g in range(kv_local):
            vals_t[g] = own_ref[g, 1].T

    seen = own_seen(seg, tlen, lanes, group)
    for g in range(kv_local):
        score = jnp.where(seen, dot(own_ref[g, 0], q_ref[g, 0], NT), -jnp.inf)
        top = jnp.max(score, axis=0, keepdims=True)
        weight = jnp.exp2((score - top) * rate)
        stat_ref[g, 0, 0:1, :] = top
        stat_ref[g, 0, 1:2, :] = jnp.sum(weight, axis=0, keepdims=True)
        part_ref[g, 0] = dot(vals_t[g], weight.astype(BF16), NN)


def seg_spec(kv_local, rows, columns):
    return pl.BlockSpec((kv_local, 1, rows, columns), lambda s: (0, s, 0, 0))


def attend_own(q, own):
    kv_local, nseg, block, hdim = q.shape
    tlen = own.shape[2]
    return pl.pallas_call(
        functools.partial(own_kernel, block // SEG, 1.0 / (math.sqrt(hdim) * math.log(2.0))),
        grid=(nseg,),
        out_shape=(
            jax.ShapeDtypeStruct((kv_local, nseg, 8, block), F32),
            jax.ShapeDtypeStruct((kv_local, nseg, hdim, block), F32),
        ),
        in_specs=[
            seg_spec(kv_local, block, hdim),
            pl.BlockSpec(own.shape, lambda s: (0, 0, 0, 0)),
        ],
        out_specs=(seg_spec(kv_local, 8, block), seg_spec(kv_local, hdim, block)),
        scratch_shapes=[pltpu.VMEM((kv_local, hdim, tlen), BF16)],
        compiler_params=params(32),
        cost_estimate=cost(kv_local, nseg, block, tlen, hdim, 2),
    )(q, own)


def docs_kernel(
    docs_dev, rate, scale, depth,
    cit_ref, slot_ref, vis_ref, q_ref, do_ref, stat_ref, own_ref, arr_ref,
    out_hbm, final_hbm, keys_hbm, vals_hbm, part_hbm,
    keys, vals, vals_t, dkey, dval, out_ref, final_ref, part_ref, sems, out_sems, part_sems,
):
    me = lax.axis_index("dp")
    cites = cit_ref.shape[0]
    kv_local, nseg, _, hdim = q_ref.shape
    _, nhead, _, dlen_local, _ = arr_ref.shape
    dlen = nhead * dlen_local
    owners = [lax.div(slot_ref[cit_ref[c, me]], docs_dev) for c in range(cites)]
    for c in range(cites):
        rows = pl.ds(c * dlen, dlen)
        for g in range(kv_local):
            keys[g, rows, :] = arr_ref[owners[c], :, 2 * g].reshape(dlen, hdim)
            value = arr_ref[owners[c], :, 2 * g + 1].reshape(dlen, hdim)
            vals[g, rows, :] = value
            vals_t[g, :, rows] = value.T
    copies = [
        pltpu.make_async_copy(keys, keys_hbm, sems.at[0]),
        pltpu.make_async_copy(vals, vals_hbm, sems.at[1]),
    ]
    for copy in copies:
        copy.start()

    def add(ref, g, seg, term):
        ref[g] = term if seg == 0 else ref[g] + term

    def stages(g, seg):
        q = q_ref[g, seg]
        do = do_ref[g, seg]
        score = dot(keys[g], q, NT)
        yield
        own_top = stat_ref[g, seg, 0:1, :]
        top = own_top
        tops = []
        sums = []
        weights = []
        for c in range(cites):
            part = score[c * dlen : (c + 1) * dlen]
            doc_top = jnp.max(part, axis=0, keepdims=True)
            weights.append(jnp.exp2((part - doc_top) * rate))
            sums.append(jnp.sum(weights[-1], axis=0, keepdims=True))
            tops.append(jnp.where(vis_ref[0, c] <= seg, doc_top, -jnp.inf))
            top = jnp.maximum(top, tops[-1])
        own_factor = jnp.exp2((own_top - top) * rate)
        factors = [jnp.exp2((t - top) * rate) for t in tops]
        total = stat_ref[g, seg, 1:2, :] * own_factor
        for f, s in zip(factors, sums):
            total = total + f * s
        inverse = 1.0 / total
        prob = jnp.concatenate([(w * (f * inverse)).astype(BF16) for w, f in zip(weights, factors)], 0)
        yield
        out = own_ref[g, seg] * (own_factor * inverse) + dot(vals_t[g], prob, NN)
        add(dval, g, seg, dot(prob, do, NN))
        out = out.astype(BF16)
        out_ref[g, seg] = out
        copies.append(
            pltpu.make_async_copy(out_ref.at[g, seg], out_hbm.at[g, seg], out_sems.at[g * nseg + seg])
        )
        copies[-1].start()
        yield
        delta = jnp.sum(do.T.astype(F32) * out.astype(F32), axis=0, keepdims=True)
        final_ref[g, seg, 0:1, :] = top
        final_ref[g, seg, 1:2, :] = inverse
        final_ref[g, seg, 2:3, :] = delta
        dprob = dot(vals[g], do, NT)
        dscore = (prob.astype(F32) * (dprob - delta)).astype(BF16)
        yield
        add(dkey, g, seg, dot(dscore, q, NN))

    waiting = [stages(g, seg) for seg in range(nseg) for g in range(kv_local)]
    active = []
    while waiting or active:
        if waiting and len(active) < depth:
            active.append(waiting.pop(0))
        active = [item for item in active if next(item, "end") != "end"]

    shape = (nhead, dlen_local, hdim)
    for c in range(cites):
        rows = pl.ds(c * dlen, dlen)
        for g in range(kv_local):
            part_ref[c, :, 2 * g] = (dkey[g, rows, :] * scale).astype(BF16).reshape(shape)
            part_ref[c, :, 2 * g + 1] = dval[g, rows, :].astype(BF16).reshape(shape)
        copies.append(pltpu.make_async_copy(part_ref.at[c], part_hbm.at[owners[c]], part_sems.at[c]))
        copies[-1].start()
    copies.append(pltpu.make_async_copy(final_ref, final_hbm, sems.at[2]))
    copies[-1].start()
    for copy in copies:
        copy.wait()


def attend_docs(cit, doc_slot, visible_from, q, do, stat, own_part, arrived, docs_dev):
    kv_local, nseg, block, hdim = q.shape
    cites = cit.shape[0]
    _, nhead, per, dlen_local, _ = arrived.shape
    ndoc = cites * nhead * dlen_local
    rate = 1.0 / (math.sqrt(hdim) * math.log(2.0))
    depth = 5 if ndoc <= 512 else 1

    return pl.pallas_call(
        functools.partial(docs_kernel, docs_dev, rate, 1.0 / math.sqrt(hdim), depth),
        out_shape=(
            jax.ShapeDtypeStruct((kv_local, nseg, hdim, block), BF16),
            jax.ShapeDtypeStruct((kv_local, nseg, 8, block), F32),
            jax.ShapeDtypeStruct((kv_local, ndoc, hdim), BF16),
            jax.ShapeDtypeStruct((kv_local, ndoc, hdim), BF16),
            jax.ShapeDtypeStruct(arrived.shape, BF16),
        ),
        in_specs=[SMEM, SMEM, SMEM, VMEM, VMEM, VMEM, VMEM, VMEM],
        out_specs=(HBM, HBM, HBM, HBM, HBM),
        scratch_shapes=[
            pltpu.VMEM((kv_local, ndoc, hdim), BF16),
            pltpu.VMEM((kv_local, ndoc, hdim), BF16),
            pltpu.VMEM((kv_local, hdim, ndoc), BF16),
            pltpu.VMEM((kv_local, ndoc, hdim), F32),
            pltpu.VMEM((kv_local, ndoc, hdim), F32),
            pltpu.VMEM((kv_local, nseg, hdim, block), BF16),
            pltpu.VMEM((kv_local, nseg, 8, block), F32),
            pltpu.VMEM((cites,) + arrived.shape[1:], BF16),
            pltpu.SemaphoreType.DMA((3,)),
            pltpu.SemaphoreType.DMA((kv_local * nseg,)),
            pltpu.SemaphoreType.DMA((cites,)),
        ],
        compiler_params=params(40),
        cost_estimate=cost(kv_local, nseg, block, ndoc, hdim, 5),
    )(scalar(cit), scalar(doc_slot), scalar(visible_from), near(q), near(do), near(stat), near(own_part), near(arrived))


def rest_kernel(
    group, rate, scale,
    vis_ref, q_ref, do_ref, own_ref, dockeys_ref, docvals_ref, out_ref, final_ref,
    o_ref, dq_ref, down_ref,
    keys, vals, keys_t, dkey, dval,
):
    seg = pl.program_id(0)
    last = pl.num_programs(0) - 1
    kv_local, _, lanes, _ = q_ref.shape
    ndoc = dockeys_ref.shape[1]
    cites = vis_ref.shape[1]
    dlen = ndoc // cites
    tlen = own_ref.shape[2]

    @pl.when(seg == 0)
    def _():
        dkey[...] = jnp.zeros_like(dkey)
        dval[...] = jnp.zeros_like(dval)
        for g in range(kv_local):
            keys[g, :ndoc, :] = dockeys_ref[g]
            vals[g, :ndoc, :] = docvals_ref[g]
            keys[g, ndoc:, :] = own_ref[g, 0]
            vals[g, ndoc:, :] = own_ref[g, 1]
            keys_t[g] = keys[g].T

    seen = own_seen(seg, tlen, lanes, group)
    for g in range(kv_local):
        q = q_ref[g, 0]
        do = do_ref[g, 0]
        top = final_ref[g, 0, 0:1, :]
        inverse = final_ref[g, 0, 1:2, :]
        delta = final_ref[g, 0, 2:3, :]
        score = dot(keys[g], q, NT)
        parts = [
            jnp.where(vis_ref[0, c] <= seg, score[c * dlen : (c + 1) * dlen], -jnp.inf)
            for c in range(cites)
        ]
        parts.append(jnp.where(seen, score[ndoc:], -jnp.inf))
        prob = jnp.exp2((jnp.concatenate(parts, 0) - top) * rate) * inverse
        dprob = dot(vals[g], do, NT)
        dscore = (prob * (dprob - delta)).astype(BF16)
        dkey[g] += dot(dscore[ndoc:], q, NN)
        dval[g] += dot(prob[ndoc:].astype(BF16), do, NN)
        dq_ref[g, 0] = (dot(keys_t[g], dscore, NN) * scale).astype(BF16).T
        o_ref[g, 0] = out_ref[g, 0].T

    @pl.when(seg == last)
    def _():
        down_ref[:, 0] = (dkey[...] * scale).astype(BF16)
        down_ref[:, 1] = dval[...].astype(BF16)


def attend_rest(visible_from, q, do, own, doc_keys, doc_vals, out_t, final):
    kv_local, nseg, block, hdim = q.shape
    tlen = own.shape[2]
    total = doc_keys.shape[1] + tlen
    row_spec = seg_spec(kv_local, block, hdim)
    whole_own = pl.BlockSpec(own.shape, lambda s: (0, 0, 0, 0))
    whole_doc = pl.BlockSpec(doc_keys.shape, lambda s: (0, 0, 0))
    rate = 1.0 / (math.sqrt(hdim) * math.log(2.0))
    return pl.pallas_call(
        functools.partial(rest_kernel, block // SEG, rate, 1.0 / math.sqrt(hdim)),
        grid=(nseg,),
        out_shape=(
            jax.ShapeDtypeStruct(q.shape, BF16),
            jax.ShapeDtypeStruct(q.shape, BF16),
            jax.ShapeDtypeStruct(own.shape, BF16),
        ),
        in_specs=[
            SMEM, row_spec, row_spec, whole_own, whole_doc, whole_doc,
            seg_spec(kv_local, hdim, block), seg_spec(kv_local, 8, block),
        ],
        out_specs=(row_spec, row_spec, whole_own),
        scratch_shapes=[
            pltpu.VMEM((kv_local, total, hdim), BF16),
            pltpu.VMEM((kv_local, total, hdim), BF16),
            pltpu.VMEM((kv_local, hdim, total), BF16),
            pltpu.VMEM((kv_local, tlen, hdim), F32),
            pltpu.VMEM((kv_local, tlen, hdim), F32),
        ],
        compiler_params=params(40),
        cost_estimate=cost(kv_local, nseg, block, 3 * total, hdim),
    )(visible_from, q, do, own, doc_keys, doc_vals, out_t, final)


def settle_kernel(cit_ref, slot_ref, got_ref, out_ref, total, turned, sems):
    me = lax.axis_index("dp")
    ntraj, nhead, per, dlen_local, hdim = got_ref.shape
    cites = cit_ref.shape[0]
    docs_dev = out_ref.shape[0]
    places = [place_of(cit_ref, slot_ref, t, cites, docs_dev, me) for t in range(ntraj)]
    stores = []
    for d in range(docs_dev):
        total[d] = jnp.zeros_like(total[d])
        for t in range(ntraj):

            @pl.when(places[t] == d)
            def _():
                total[d] += got_ref[t].astype(F32)

        turned[d] = jnp.swapaxes(total[d].reshape(nhead * per, dlen_local, hdim), 0, 1)
        stores.append(pltpu.make_async_copy(turned.at[d], out_ref.at[d], sems.at[d]))
        stores[-1].start()
    for store in stores:
        store.wait()


def settle(cit, doc_slot, got, docs_dev):
    _, nhead, per, dlen_local, hdim = got.shape
    return pl.pallas_call(
        settle_kernel,
        out_shape=jax.ShapeDtypeStruct((docs_dev, dlen_local, nhead * per, hdim), F32),
        in_specs=[SMEM, SMEM, VMEM],
        out_specs=HBM,
        scratch_shapes=[
            pltpu.VMEM((docs_dev, nhead, per, dlen_local, hdim), F32),
            pltpu.VMEM((docs_dev, dlen_local, nhead * per, hdim), F32),
            pltpu.SemaphoreType.DMA((docs_dev,)),
        ],
        compiler_params=params(32),
    )(scalar(cit), scalar(doc_slot), near(got))


def body(queries, traj_kv, grad_out, doc_kv, citations, doc_slot, visible_from):
    nhead = lax.axis_size("head")
    ndp = lax.axis_size("dp")
    tlen, heads_local, hdim = queries.shape
    kv_local = traj_kv.shape[1]
    group = heads_local // kv_local
    docs_dev, dlen_local = doc_kv.shape[:2]
    per = kv_local * 2
    cit = citations.T
    outgoing = pack(cit, doc_slot, doc_kv, nhead)
    arrived = lax.all_to_all(outgoing, ("dp", "head"), split_axis=0, concat_axis=0, tiled=True)
    arrived = arrived.reshape(ndp, nhead, per, dlen_local, hdim)

    def by_kv(x):
        x = x.reshape(tlen, kv_local, group, hdim).transpose(1, 0, 2, 3)
        return x.reshape(kv_local, tlen // SEG, SEG * group, hdim)

    def by_token(x):
        x = x.reshape(kv_local, tlen, group, hdim).transpose(1, 0, 2, 3)
        return x.reshape(tlen, heads_local, hdim)

    q = by_kv(queries)
    do = by_kv(grad_out)
    own = traj_kv.transpose(1, 2, 0, 3)
    stat, own_part = attend_own(q, own)
    out_t, final, doc_keys, doc_vals, part = attend_docs(
        cit, doc_slot, visible_from, q, do, stat, own_part, arrived, docs_dev
    )
    got = lax.all_to_all(
        part.reshape(outgoing.shape), ("dp", "head"), split_axis=0, concat_axis=0, tiled=True
    )
    attended, d_queries, d_own = attend_rest(
        visible_from, q, do, own, doc_keys, doc_vals, out_t, final
    )
    d_doc = settle(cit, doc_slot, got.reshape(ndp, nhead, per, dlen_local, hdim), docs_dev)
    return (
        by_token(attended),
        by_token(d_queries),
        d_own.transpose(2, 0, 1, 3),
        d_doc.reshape(docs_dev, dlen_local, nhead * kv_local, 2, hdim),
    )


def solution(mesh):
    in_specs = (
        P("dp", "head", None),
        P("dp", "head", None, None),
        P("dp", "head", None),
        P("dp", "head", None, None, None),
        P(),
        P(),
        P("dp", None),
    )
    out_specs = (
        P("dp", "head", None),
        P("dp", "head", None),
        P("dp", "head", None, None),
        P("dp", "head", None, None, None),
    )
    return jax.shard_map(body, mesh=mesh, in_specs=in_specs, out_specs=out_specs, check_vma=False)
```

```python
import functools
import math

import jax
import jax.numpy as jnp
from jax import lax
from jax.experimental import pallas as pl
from jax.experimental.pallas import tpu as pltpu
from jax.sharding import PartitionSpec as P

SEG = 64
BF16 = jnp.bfloat16
F32 = jnp.float32
NT = (((1,), (1,)), ((), ()))
NN = (((1,), (0,)), ((), ()))
SMEM = pl.BlockSpec(memory_space=pltpu.SMEM)
VMEM = pl.BlockSpec(memory_space=pltpu.VMEM)
HBM = pl.BlockSpec(memory_space=pltpu.HBM)


def dot(a, b, dims):
    return lax.dot_general(a, b, dims, preferred_element_type=F32)


def params(megabytes):
    return pltpu.CompilerParams(vmem_limit_bytes=megabytes * 1024 * 1024)


def cost(*shape):
    flops = 2 * math.prod(shape)
    return pl.CostEstimate(flops=flops, bytes_accessed=8 * 1024 * 1024, transcendentals=0)


def near(x):
    return pltpu.with_memory_space_constraint(x, pltpu.VMEM)


def scalar(x):
    return pltpu.with_memory_space_constraint(x, pltpu.SMEM)


def place_of(cit_ref, slot_ref, t, cites, docs_dev, me):
    place = jnp.int32(-1)
    for c in range(cites):
        slot = slot_ref[cit_ref[c, t]]
        place = jnp.where(lax.div(slot, docs_dev) == me, lax.rem(slot, docs_dev), place)
    return place


def pack_kernel(cit_hbm, slot_hbm, doc_ref, out_ref, cit_ref, slot_ref, held, turned, in_sems, out_sems):
    me = lax.axis_index("dp")
    cites, ntraj = cit_ref.shape
    docs_dev = doc_ref.shape[0]
    scalars = [
        pltpu.make_async_copy(cit_hbm, cit_ref, in_sems.at[docs_dev]),
        pltpu.make_async_copy(slot_hbm, slot_ref, in_sems.at[docs_dev + 1]),
    ]
    for load in scalars:
        load.start()
    loads = [pltpu.make_async_copy(doc_ref.at[d], held.at[d], in_sems.at[d]) for d in range(docs_dev)]
    for load in loads:
        load.start()
    for load in scalars:
        load.wait()
    places = [place_of(cit_ref, slot_ref, t, cites, docs_dev, me) for t in range(ntraj)]
    for d in range(docs_dev):
        loads[d].wait()
        turned[d] = jnp.swapaxes(held[d].astype(F32), 0, 1).astype(BF16)
    stores = []
    for t in range(ntraj):
        source = turned.at[jnp.maximum(places[t], 0)]
        stores.append(pltpu.make_async_copy(source, out_ref.at[t], out_sems.at[t]))
        stores[-1].start()
    for store in stores:
        store.wait()


def pack(cit, doc_slot, doc_kv, nhead):
    docs_dev, dlen_local, kv, two, hdim = doc_kv.shape
    ntraj = cit.shape[1]
    rows = kv * two
    out = pl.pallas_call(
        pack_kernel,
        out_shape=jax.ShapeDtypeStruct((ntraj, rows, dlen_local, hdim), BF16),
        in_specs=[HBM, HBM, HBM],
        out_specs=HBM,
        scratch_shapes=[
            pltpu.SMEM(cit.shape, jnp.int32),
            pltpu.SMEM(doc_slot.shape, jnp.int32),
            pltpu.VMEM((docs_dev, dlen_local, rows, hdim), BF16),
            pltpu.VMEM((docs_dev, rows, dlen_local, hdim), BF16),
            pltpu.SemaphoreType.DMA((docs_dev + 2,)),
            pltpu.SemaphoreType.DMA((ntraj,)),
        ],
        compiler_params=params(60),
    )(cit, doc_slot, doc_kv.reshape(docs_dev, dlen_local, rows, hdim))
    return out.reshape(ntraj * nhead, rows // nhead, dlen_local, hdim)


def own_seen(seg, tlen, lanes, group):
    key = lax.broadcasted_iota(jnp.int32, (tlen, lanes), 0)
    token = seg * SEG + lax.broadcasted_iota(jnp.int32, (tlen, lanes), 1) // group
    return key <= token


def own_kernel(group, rate, q_ref, own_ref, stat_ref, part_ref, vals_t):
    seg = pl.program_id(0)
    kv_local, _, lanes, _ = q_ref.shape
    tlen = own_ref.shape[2]

    @pl.when(seg == 0)
    def _():
        for g in range(kv_local):
            vals_t[g] = own_ref[g, 1].T

    seen = own_seen(seg, tlen, lanes, group)
    for g in range(kv_local):
        score = jnp.where(seen, dot(own_ref[g, 0], q_ref[g, 0], NT), -jnp.inf)
        top = jnp.max(score, axis=0, keepdims=True)
        weight = jnp.exp2((score - top) * rate)
        stat_ref[g, 0, 0:1, :] = top
        stat_ref[g, 0, 1:2, :] = jnp.sum(weight, axis=0, keepdims=True)
        part_ref[g, 0] = dot(vals_t[g], weight.astype(BF16), NN)


def seg_spec(kv_local, rows, columns):
    return pl.BlockSpec((kv_local, 1, rows, columns), lambda s: (0, s, 0, 0))


def attend_own(q, own):
    kv_local, nseg, block, hdim = q.shape
    tlen = own.shape[2]
    return pl.pallas_call(
        functools.partial(own_kernel, block // SEG, 1.0 / (math.sqrt(hdim) * math.log(2.0))),
        grid=(nseg,),
        out_shape=(
            pltpu.VMEM((kv_local, nseg, 8, block), F32),
            pltpu.VMEM((kv_local, nseg, hdim, block), F32),
        ),
        in_specs=[
            seg_spec(kv_local, block, hdim),
            pl.BlockSpec(own.shape, lambda s: (0, 0, 0, 0)),
        ],
        out_specs=(seg_spec(kv_local, 8, block), seg_spec(kv_local, hdim, block)),
        scratch_shapes=[pltpu.VMEM((kv_local, hdim, tlen), BF16)],
        compiler_params=params(32),
        cost_estimate=cost(kv_local, nseg, block, tlen, hdim, 2),
    )(q, own)


def docs_kernel(
    docs_dev, rate, scale, depth,
    cit_ref, slot_ref, vis_ref, q_ref, do_ref, stat_ref, own_ref, arr_ref,
    part_hbm,
    keys, vals, vals_t, dkey, dval, part_ref, sems,
):
    me = lax.axis_index("dp")
    cites = cit_ref.shape[0]
    kv_local, nseg, _, hdim = q_ref.shape
    _, nhead, _, dlen_local, _ = arr_ref.shape
    dlen = nhead * dlen_local
    owners = [lax.div(slot_ref[cit_ref[c, me]], docs_dev) for c in range(cites)]
    for c in range(cites):
        rows = pl.ds(c * dlen, dlen)
        for g in range(kv_local):
            keys[g, rows, :] = arr_ref[owners[c], :, 2 * g].reshape(dlen, hdim)
            value = arr_ref[owners[c], :, 2 * g + 1].reshape(dlen, hdim)
            vals[g, rows, :] = value
            vals_t[g, :, rows] = value.T

    def add(ref, g, seg, term):
        ref[g] = term if seg == 0 else ref[g] + term

    def stages(g, seg):
        q = q_ref[g, seg]
        do = do_ref[g, seg]
        score = dot(keys[g], q, NT)
        yield
        own_top = stat_ref[g, seg, 0:1, :]
        top = own_top
        tops = []
        sums = []
        weights = []
        for c in range(cites):
            part = score[c * dlen : (c + 1) * dlen]
            doc_top = jnp.max(part, axis=0, keepdims=True)
            weights.append(jnp.exp2((part - doc_top) * rate))
            sums.append(jnp.sum(weights[-1], axis=0, keepdims=True))
            tops.append(jnp.where(vis_ref[0, c] <= seg, doc_top, -jnp.inf))
            top = jnp.maximum(top, tops[-1])
        own_factor = jnp.exp2((own_top - top) * rate)
        factors = [jnp.exp2((t - top) * rate) for t in tops]
        total = stat_ref[g, seg, 1:2, :] * own_factor
        for f, s in zip(factors, sums):
            total = total + f * s
        inverse = 1.0 / total
        prob = jnp.concatenate([(w * (f * inverse)).astype(BF16) for w, f in zip(weights, factors)], 0)
        yield
        out = own_ref[g, seg] * (own_factor * inverse) + dot(vals_t[g], prob, NN)
        add(dval, g, seg, dot(prob, do, NN))
        out = out.astype(BF16)
        yield
        delta = jnp.sum(do.T.astype(F32) * out.astype(F32), axis=0, keepdims=True)
        dprob = dot(vals[g], do, NT)
        dscore = (prob.astype(F32) * (dprob - delta)).astype(BF16)
        yield
        add(dkey, g, seg, dot(dscore, q, NN))

    waiting = [stages(g, seg) for seg in range(nseg) for g in range(kv_local)]
    active = []
    while waiting or active:
        if waiting and len(active) < depth:
            active.append(waiting.pop(0))
        active = [item for item in active if next(item, "end") != "end"]

    shape = (nhead, dlen_local, hdim)
    copies = []
    for c in range(cites):
        rows = pl.ds(c * dlen, dlen)
        for g in range(kv_local):
            part_ref[c, :, 2 * g] = (dkey[g, rows, :] * scale).astype(BF16).reshape(shape)
            part_ref[c, :, 2 * g + 1] = dval[g, rows, :].astype(BF16).reshape(shape)
        copies.append(pltpu.make_async_copy(part_ref.at[c], part_hbm.at[owners[c]], sems.at[c]))
        copies[-1].start()
    for copy in copies:
        copy.wait()


def attend_docs(cit, doc_slot, visible_from, q, do, stat, own_part, arrived, docs_dev):
    kv_local, nseg, block, hdim = q.shape
    cites = cit.shape[0]
    _, nhead, per, dlen_local, _ = arrived.shape
    ndoc = cites * nhead * dlen_local
    rate = 1.0 / (math.sqrt(hdim) * math.log(2.0))
    depth = 5 if ndoc <= 512 else 1

    return pl.pallas_call(
        functools.partial(docs_kernel, docs_dev, rate, 1.0 / math.sqrt(hdim), depth),
        out_shape=pltpu.HBM(arrived.shape, BF16),
        in_specs=[SMEM, SMEM, SMEM, VMEM, VMEM, VMEM, VMEM, VMEM],
        out_specs=HBM,
        scratch_shapes=[
            pltpu.VMEM((kv_local, ndoc, hdim), BF16),
            pltpu.VMEM((kv_local, ndoc, hdim), BF16),
            pltpu.VMEM((kv_local, hdim, ndoc), BF16),
            pltpu.VMEM((kv_local, ndoc, hdim), F32),
            pltpu.VMEM((kv_local, ndoc, hdim), F32),
            pltpu.VMEM((cites,) + arrived.shape[1:], BF16),
            pltpu.SemaphoreType.DMA((cites,)),
        ],
        compiler_params=params(40),
        cost_estimate=cost(kv_local, nseg, block, ndoc, hdim, 5),
    )(scalar(cit), scalar(doc_slot), scalar(visible_from), near(q), near(do), near(stat), near(own_part), near(arrived))


def rest_kernel(
    docs_dev, group, rate, scale,
    cit_ref, slot_ref, vis_ref, q_ref, do_ref, own_ref, arr_ref,
    o_ref, dq_ref, down_ref,
    held, keys, vals, keys_t, vals_t, dkey, dval, sems,
):
    seg = pl.program_id(0)
    last = pl.num_programs(0) - 1
    me = lax.axis_index("dp")
    kv_local, _, lanes, hdim = q_ref.shape
    cites, nhead, _, dlen_local, _ = held.shape
    dlen = nhead * dlen_local
    ndoc = cites * dlen
    tlen = own_ref.shape[2]

    def fetch(c):
        owner = lax.div(slot_ref[cit_ref[c, me]], docs_dev)
        return pltpu.make_async_copy(arr_ref.at[owner], held.at[c], sems.at[c])

    @pl.when(seg == 0)
    def _():
        for c in range(cites):
            fetch(c).start()
        dkey[...] = jnp.zeros_like(dkey)
        dval[...] = jnp.zeros_like(dval)
        for c in range(cites):
            fetch(c).wait()
            rows = pl.ds(c * dlen, dlen)
            for g in range(kv_local):
                keys[g, rows, :] = held[c, :, 2 * g].reshape(dlen, hdim)
                vals[g, rows, :] = held[c, :, 2 * g + 1].reshape(dlen, hdim)
        for g in range(kv_local):
            keys[g, ndoc:, :] = own_ref[g, 0]
            vals[g, ndoc:, :] = own_ref[g, 1]
            keys_t[g] = keys[g].T
            vals_t[g] = vals[g].T

    seen = own_seen(seg, tlen, lanes, group)
    for g in range(kv_local):
        q = q_ref[g, 0]
        do = do_ref[g, 0]
        score = dot(keys[g], q, NT)
        parts = [
            jnp.where(vis_ref[0, c] <= seg, score[c * dlen : (c + 1) * dlen], -jnp.inf)
            for c in range(cites)
        ]
        parts.append(jnp.where(seen, score[ndoc:], -jnp.inf))
        score = jnp.concatenate(parts, 0)
        weight = jnp.exp2((score - jnp.max(score, axis=0, keepdims=True)) * rate)
        prob = weight * (1.0 / jnp.sum(weight, axis=0, keepdims=True))
        prob16 = prob.astype(BF16)
        out = dot(vals_t[g], prob16, NN).astype(BF16)
        o_ref[g, 0] = out.T
        delta = jnp.sum(do.T.astype(F32) * out.astype(F32), axis=0, keepdims=True)
        dprob = dot(vals[g], do, NT)
        dscore = (prob * (dprob - delta)).astype(BF16)
        dkey[g] += dot(dscore[ndoc:], q, NN)
        dval[g] += dot(prob16[ndoc:], do, NN)
        dq_ref[g, 0] = (dot(keys_t[g], dscore, NN) * scale).astype(BF16).T

    @pl.when(seg == last)
    def _():
        down_ref[:, 0] = (dkey[...] * scale).astype(BF16)
        down_ref[:, 1] = dval[...].astype(BF16)


def attend_rest(cit, doc_slot, visible_from, q, do, own, arrived, docs_dev):
    kv_local, nseg, block, hdim = q.shape
    tlen = own.shape[2]
    cites = cit.shape[0]
    _, nhead, per, dlen_local, _ = arrived.shape
    total = cites * nhead * dlen_local + tlen
    row_spec = seg_spec(kv_local, block, hdim)
    whole_own = pl.BlockSpec(own.shape, lambda s: (0, 0, 0, 0))
    rate = 1.0 / (math.sqrt(hdim) * math.log(2.0))
    return pl.pallas_call(
        functools.partial(rest_kernel, docs_dev, block // SEG, rate, 1.0 / math.sqrt(hdim)),
        grid=(nseg,),
        out_shape=(
            jax.ShapeDtypeStruct(q.shape, BF16),
            jax.ShapeDtypeStruct(q.shape, BF16),
            jax.ShapeDtypeStruct(own.shape, BF16),
        ),
        in_specs=[SMEM, SMEM, SMEM, row_spec, row_spec, whole_own, HBM],
        out_specs=(row_spec, row_spec, whole_own),
        scratch_shapes=[
            pltpu.VMEM((cites, nhead, per, dlen_local, hdim), BF16),
            pltpu.VMEM((kv_local, total, hdim), BF16),
            pltpu.VMEM((kv_local, total, hdim), BF16),
            pltpu.VMEM((kv_local, hdim, total), BF16),
            pltpu.VMEM((kv_local, hdim, total), BF16),
            pltpu.VMEM((kv_local, tlen, hdim), F32),
            pltpu.VMEM((kv_local, tlen, hdim), F32),
            pltpu.SemaphoreType.DMA((cites,)),
        ],
        compiler_params=params(40),
        cost_estimate=cost(kv_local, nseg, block, 3 * total, hdim),
    )(cit, doc_slot, visible_from, q, do, own, arrived)


def settle_kernel(cit_ref, slot_ref, got_ref, out_ref, total, turned, sems):
    me = lax.axis_index("dp")
    ntraj, nhead, per, dlen_local, hdim = got_ref.shape
    cites = cit_ref.shape[0]
    docs_dev = out_ref.shape[0]
    places = [place_of(cit_ref, slot_ref, t, cites, docs_dev, me) for t in range(ntraj)]
    stores = []
    for d in range(docs_dev):
        total[d] = jnp.zeros_like(total[d])
        for t in range(ntraj):

            @pl.when(places[t] == d)
            def _():
                total[d] += got_ref[t].astype(F32)

        turned[d] = jnp.swapaxes(total[d].reshape(nhead * per, dlen_local, hdim), 0, 1)
        stores.append(pltpu.make_async_copy(turned.at[d], out_ref.at[d], sems.at[d]))
        stores[-1].start()
    for store in stores:
        store.wait()


def settle(cit, doc_slot, got, docs_dev):
    _, nhead, per, dlen_local, hdim = got.shape
    return pl.pallas_call(
        settle_kernel,
        out_shape=jax.ShapeDtypeStruct((docs_dev, dlen_local, nhead * per, hdim), F32),
        in_specs=[SMEM, SMEM, VMEM],
        out_specs=HBM,
        scratch_shapes=[
            pltpu.VMEM((docs_dev, nhead, per, dlen_local, hdim), F32),
            pltpu.VMEM((docs_dev, dlen_local, nhead * per, hdim), F32),
            pltpu.SemaphoreType.DMA((docs_dev,)),
        ],
        compiler_params=params(32),
    )(scalar(cit), scalar(doc_slot), near(got))


def body(queries, traj_kv, grad_out, doc_kv, citations, doc_slot, visible_from):
    nhead = lax.axis_size("head")
    ndp = lax.axis_size("dp")
    tlen, heads_local, hdim = queries.shape
    kv_local = traj_kv.shape[1]
    group = heads_local // kv_local
    docs_dev, dlen_local = doc_kv.shape[:2]
    per = kv_local * 2
    cit = citations.T
    outgoing = pack(cit, doc_slot, doc_kv, nhead)
    arrived = lax.all_to_all(outgoing, ("dp", "head"), split_axis=0, concat_axis=0, tiled=True)
    arrived = arrived.reshape(ndp, nhead, per, dlen_local, hdim)

    def by_kv(x):
        x = x.reshape(tlen, kv_local, group, hdim).transpose(1, 0, 2, 3)
        return x.reshape(kv_local, tlen // SEG, SEG * group, hdim)

    def by_token(x):
        x = x.reshape(kv_local, tlen, group, hdim).transpose(1, 0, 2, 3)
        return x.reshape(tlen, heads_local, hdim)

    q = by_kv(queries)
    do = by_kv(grad_out)
    own = traj_kv.transpose(1, 2, 0, 3)
    stat, own_part = attend_own(q, own)
    part = attend_docs(cit, doc_slot, visible_from, q, do, stat, own_part, arrived, docs_dev)
    part, q, do, arrived = lax.optimization_barrier((part, q, do, arrived))
    got = lax.all_to_all(
        part.reshape(outgoing.shape), ("dp", "head"), split_axis=0, concat_axis=0, tiled=True
    )
    attended, d_queries, d_own = attend_rest(
        cit, doc_slot, visible_from, q, do, own, arrived, docs_dev
    )
    d_doc = settle(cit, doc_slot, got.reshape(ndp, nhead, per, dlen_local, hdim), docs_dev)
    return (
        by_token(attended),
        by_token(d_queries),
        d_own.transpose(2, 0, 1, 3),
        d_doc.reshape(docs_dev, dlen_local, nhead * kv_local, 2, hdim),
    )


def solution(mesh):
    in_specs = (
        P("dp", "head", None),
        P("dp", "head", None, None),
        P("dp", "head", None),
        P("dp", "head", None, None, None),
        P(),
        P(),
        P("dp", None),
    )
    out_specs = (
        P("dp", "head", None),
        P("dp", "head", None),
        P("dp", "head", None, None),
        P("dp", "head", None, None, None),
    )
    return jax.shard_map(body, mesh=mesh, in_specs=in_specs, out_specs=out_specs, check_vma=False)
```

```python
import functools
import math

import jax
import jax.numpy as jnp
from jax import lax
from jax.experimental import pallas as pl
from jax.experimental.pallas import tpu as pltpu
from jax.sharding import PartitionSpec as P

SEG = 64
BF16 = jnp.bfloat16
F32 = jnp.float32
NT = (((1,), (1,)), ((), ()))
NN = (((1,), (0,)), ((), ()))
SMEM = pl.BlockSpec(memory_space=pltpu.SMEM)
VMEM = pl.BlockSpec(memory_space=pltpu.VMEM)
HBM = pl.BlockSpec(memory_space=pltpu.HBM)


def dot(a, b, dims):
    return lax.dot_general(a, b, dims, preferred_element_type=F32)


def params(megabytes):
    return pltpu.CompilerParams(vmem_limit_bytes=megabytes * 1024 * 1024)


def cost(*shape):
    flops = 2 * math.prod(shape)
    return pl.CostEstimate(flops=flops, bytes_accessed=8 * 1024 * 1024, transcendentals=0)


def near(x):
    return pltpu.with_memory_space_constraint(x, pltpu.VMEM)


def scalar(x):
    return pltpu.with_memory_space_constraint(x, pltpu.SMEM)


def place_of(cit_ref, slot_ref, t, cites, docs_dev, me):
    place = jnp.int32(-1)
    for c in range(cites):
        slot = slot_ref[cit_ref[c, t]]
        place = jnp.where(lax.div(slot, docs_dev) == me, lax.rem(slot, docs_dev), place)
    return place


def pack_kernel(
    cit_hbm, slot_hbm, vis_hbm, doc_ref, out_ref, table_ref,
    cit_ref, slot_ref, vis_ref, held, turned, in_sems, out_sems,
):
    me = lax.axis_index("dp")
    cites, ntraj = cit_ref.shape
    docs_dev = doc_ref.shape[0]
    scalars = [
        pltpu.make_async_copy(cit_hbm, cit_ref, in_sems.at[docs_dev]),
        pltpu.make_async_copy(slot_hbm, slot_ref, in_sems.at[docs_dev + 1]),
        pltpu.make_async_copy(vis_hbm, vis_ref, in_sems.at[docs_dev + 2]),
    ]
    for load in scalars:
        load.start()
    loads = [pltpu.make_async_copy(doc_ref.at[d], held.at[d], in_sems.at[d]) for d in range(docs_dev)]
    for load in loads:
        load.start()
    for load in scalars:
        load.wait()
    places = [place_of(cit_ref, slot_ref, t, cites, docs_dev, me) for t in range(ntraj)]
    for d in range(docs_dev):
        loads[d].wait()
        turned[d] = jnp.swapaxes(held[d].astype(F32), 0, 1).astype(BF16)
    stores = []
    for t in range(ntraj):
        source = turned.at[jnp.maximum(places[t], 0)]
        stores.append(pltpu.make_async_copy(source, out_ref.at[t], out_sems.at[t]))
        stores[-1].start()
        table_ref[2 * cites + t] = places[t]
    for c in range(cites):
        table_ref[c] = lax.div(slot_ref[cit_ref[c, me]], docs_dev)
        table_ref[cites + c] = vis_ref[0, c]
    for store in stores:
        store.wait()


def pack(cit, doc_slot, visible_from, doc_kv, nhead):
    docs_dev, dlen_local, kv, two, hdim = doc_kv.shape
    cites, ntraj = cit.shape
    rows = kv * two
    out, table = pl.pallas_call(
        pack_kernel,
        out_shape=(
            pltpu.HBM((ntraj, rows, dlen_local, hdim), BF16),
            pltpu.SMEM((2 * cites + ntraj,), jnp.int32),
        ),
        in_specs=[HBM, HBM, HBM, HBM],
        out_specs=(HBM, SMEM),
        scratch_shapes=[
            pltpu.SMEM(cit.shape, jnp.int32),
            pltpu.SMEM(doc_slot.shape, jnp.int32),
            pltpu.SMEM(visible_from.shape, jnp.int32),
            pltpu.VMEM((docs_dev, dlen_local, rows, hdim), BF16),
            pltpu.VMEM((docs_dev, rows, dlen_local, hdim), BF16),
            pltpu.SemaphoreType.DMA((docs_dev + 3,)),
            pltpu.SemaphoreType.DMA((ntraj,)),
        ],
        compiler_params=params(60),
    )(cit, doc_slot, visible_from, doc_kv.reshape(docs_dev, dlen_local, rows, hdim))
    return out.reshape(ntraj * nhead, rows // nhead, dlen_local, hdim), table


def own_seen(seg, tlen, lanes, group):
    key = lax.broadcasted_iota(jnp.int32, (tlen, lanes), 0)
    token = seg * SEG + lax.broadcasted_iota(jnp.int32, (tlen, lanes), 1) // group
    return key <= token


def seg_spec(kv_local, rows, columns):
    return pl.BlockSpec((kv_local, 1, rows, columns), lambda s: (0, s, 0, 0))


def docs_kernel(
    cites, rate, scale, depth,
    table_ref, q_ref, do_ref, own_ref, arr_ref,
    part_hbm,
    keys, vals, vals_t, own_t, dkey, dval, part_ref, sems,
):
    kv_local, nseg, lanes, hdim = q_ref.shape
    _, nhead, _, dlen_local, _ = arr_ref.shape
    dlen = nhead * dlen_local
    owners = [table_ref[c] for c in range(cites)]
    for g in range(kv_local):
        own_t[g] = own_ref[g, 1].T
        for c in range(cites):
            rows = pl.ds(c * dlen, dlen)
            keys[g, rows, :] = arr_ref[owners[c], :, 2 * g].reshape(dlen, hdim)
            value = arr_ref[owners[c], :, 2 * g + 1].reshape(dlen, hdim)
            vals[g, rows, :] = value
            vals_t[g, :, rows] = value.T

    def add(ref, g, seg, term):
        ref[g] = term if seg == 0 else ref[g] + term

    def stages(g, seg):
        q = q_ref[g, seg]
        do = do_ref[g, seg]
        before = seg * SEG
        score = dot(keys[g], q, NT)
        own = dot(own_ref[g, 0, : before + SEG], q, NT)
        yield
        seen = own_seen(0, SEG, lanes, lanes // SEG)
        edge = jnp.where(seen, own[before:], -jnp.inf)
        own = jnp.concatenate([own[:before], edge], 0) if before else edge
        own_top = jnp.max(own, axis=0, keepdims=True)
        own_weight = jnp.exp2((own - own_top) * rate)
        top = own_top
        tops = []
        sums = []
        weights = []
        for c in range(cites):
            part = score[c * dlen : (c + 1) * dlen]
            doc_top = jnp.max(part, axis=0, keepdims=True)
            weights.append(jnp.exp2((part - doc_top) * rate))
            sums.append(jnp.sum(weights[-1], axis=0, keepdims=True))
            tops.append(jnp.where(table_ref[cites + c] <= seg, doc_top, -jnp.inf))
            top = jnp.maximum(top, tops[-1])
        own_factor = jnp.exp2((own_top - top) * rate)
        factors = [jnp.exp2((t - top) * rate) for t in tops]
        total = jnp.sum(own_weight, axis=0, keepdims=True) * own_factor
        for f, s in zip(factors, sums):
            total = total + f * s
        inverse = 1.0 / total
        prob = jnp.concatenate([(w * (f * inverse)).astype(BF16) for w, f in zip(weights, factors)], 0)
        own_prob = (own_weight * (own_factor * inverse)).astype(BF16)
        yield
        out = dot(own_t[g, :, : before + SEG], own_prob, NN) + dot(vals_t[g], prob, NN)
        add(dval, g, seg, dot(prob, do, NN))
        out = out.astype(BF16)
        yield
        delta = jnp.sum(do.T.astype(F32) * out.astype(F32), axis=0, keepdims=True)
        dprob = dot(vals[g], do, NT)
        dscore = (prob.astype(F32) * (dprob - delta)).astype(BF16)
        yield
        add(dkey, g, seg, dot(dscore, q, NN))
        yield
        if seg == nseg - 1:
            give(g)

    shape = (nhead, dlen_local, hdim)
    copies = []

    def give(g):
        pair = pl.ds(2 * g, 2)
        for c in range(cites):
            rows = pl.ds(c * dlen, dlen)
            part_ref[c, :, 2 * g] = (dkey[g, rows, :] * scale).astype(BF16).reshape(shape)
            part_ref[c, :, 2 * g + 1] = dval[g, rows, :].astype(BF16).reshape(shape)
        for c in range(cites):
            source = part_ref.at[c, :, pair]
            target = part_hbm.at[owners[c], :, pair]
            copies.append(pltpu.make_async_copy(source, target, sems.at[g * cites + c]))
            copies[-1].start()

    waiting = [stages(g, seg) for seg in range(nseg) for g in range(kv_local)]
    active = []
    while waiting or active:
        if waiting and len(active) < depth:
            active.append(waiting.pop(0))
        active = [item for item in active if next(item, "end") != "end"]
    for copy in copies:
        copy.wait()


def attend_docs(table, cites, q, do, own, arrived):
    kv_local, nseg, block, hdim = q.shape
    _, nhead, per, dlen_local, _ = arrived.shape
    ndoc = cites * nhead * dlen_local
    rate = 1.0 / (math.sqrt(hdim) * math.log(2.0))
    depth = 5 if ndoc <= 512 else 1
    return pl.pallas_call(
        functools.partial(docs_kernel, cites, rate, 1.0 / math.sqrt(hdim), depth),
        out_shape=pltpu.HBM(arrived.shape, BF16),
        in_specs=[SMEM, VMEM, VMEM, VMEM, VMEM],
        out_specs=HBM,
        scratch_shapes=[
            pltpu.VMEM((kv_local, ndoc, hdim), BF16),
            pltpu.VMEM((kv_local, ndoc, hdim), BF16),
            pltpu.VMEM((kv_local, hdim, ndoc), BF16),
            pltpu.VMEM((kv_local, hdim, own.shape[2]), BF16),
            pltpu.VMEM((kv_local, ndoc, hdim), F32),
            pltpu.VMEM((kv_local, ndoc, hdim), F32),
            pltpu.VMEM((cites,) + arrived.shape[1:], BF16),
            pltpu.SemaphoreType.DMA((kv_local * cites,)),
        ],
        compiler_params=params(40),
        cost_estimate=cost(kv_local, nseg, block, ndoc, hdim, 5),
    )(scalar(table), near(q), near(do), near(own), near(arrived))


def rest_kernel(
    group, rate, scale,
    table_ref, q_ref, do_ref, own_ref, arr_ref,
    o_ref, dq_ref, down_ref,
    held, keys, vals, keys_t, vals_t, dkey, dval, sems,
):
    seg = pl.program_id(0)
    last = pl.num_programs(0) - 1
    kv_local, _, lanes, hdim = q_ref.shape
    cites, nhead, _, dlen_local, _ = held.shape
    dlen = nhead * dlen_local
    ndoc = cites * dlen
    tlen = own_ref.shape[2]

    def fetch(c):
        return pltpu.make_async_copy(arr_ref.at[table_ref[c]], held.at[c], sems.at[c])

    @pl.when(seg == 0)
    def _():
        for c in range(cites):
            fetch(c).start()
        dkey[...] = jnp.zeros_like(dkey)
        dval[...] = jnp.zeros_like(dval)
        for c in range(cites):
            fetch(c).wait()
            rows = pl.ds(c * dlen, dlen)
            for g in range(kv_local):
                keys[g, rows, :] = held[c, :, 2 * g].reshape(dlen, hdim)
                vals[g, rows, :] = held[c, :, 2 * g + 1].reshape(dlen, hdim)
        for g in range(kv_local):
            keys[g, ndoc:, :] = own_ref[g, 0]
            vals[g, ndoc:, :] = own_ref[g, 1]
            keys_t[g] = keys[g].T
            vals_t[g] = vals[g].T

    seen = own_seen(seg, tlen, lanes, group)
    for g in range(kv_local):
        q = q_ref[g, 0]
        do = do_ref[g, 0]
        score = dot(keys[g], q, NT)
        parts = [
            jnp.where(table_ref[cites + c] <= seg, score[c * dlen : (c + 1) * dlen], -jnp.inf)
            for c in range(cites)
        ]
        parts.append(jnp.where(seen, score[ndoc:], -jnp.inf))
        score = jnp.concatenate(parts, 0)
        weight = jnp.exp2((score - jnp.max(score, axis=0, keepdims=True)) * rate)
        prob = weight * (1.0 / jnp.sum(weight, axis=0, keepdims=True))
        prob16 = prob.astype(BF16)
        out = dot(vals_t[g], prob16, NN).astype(BF16)
        o_ref[g, 0] = out.T
        delta = jnp.sum(do.T.astype(F32) * out.astype(F32), axis=0, keepdims=True)
        dprob = dot(vals[g], do, NT)
        dscore = (prob * (dprob - delta)).astype(BF16)
        dkey[g] += dot(dscore[ndoc:], q, NN)
        dval[g] += dot(prob16[ndoc:], do, NN)
        dq_ref[g, 0] = (dot(keys_t[g], dscore, NN) * scale).astype(BF16).T

    @pl.when(seg == last)
    def _():
        down_ref[:, 0] = (dkey[...] * scale).astype(BF16)
        down_ref[:, 1] = dval[...].astype(BF16)


def attend_rest(table, cites, q, do, own, arrived):
    kv_local, nseg, block, hdim = q.shape
    tlen = own.shape[2]
    _, nhead, per, dlen_local, _ = arrived.shape
    total = cites * nhead * dlen_local + tlen
    row_spec = seg_spec(kv_local, block, hdim)
    whole_own = pl.BlockSpec(own.shape, lambda s: (0, 0, 0, 0))
    rate = 1.0 / (math.sqrt(hdim) * math.log(2.0))
    return pl.pallas_call(
        functools.partial(rest_kernel, block // SEG, rate, 1.0 / math.sqrt(hdim)),
        grid=(nseg,),
        out_shape=(
            jax.ShapeDtypeStruct(q.shape, BF16),
            jax.ShapeDtypeStruct(q.shape, BF16),
            jax.ShapeDtypeStruct(own.shape, BF16),
        ),
        in_specs=[SMEM, row_spec, row_spec, whole_own, HBM],
        out_specs=(row_spec, row_spec, whole_own),
        scratch_shapes=[
            pltpu.VMEM((cites, nhead, per, dlen_local, hdim), BF16),
            pltpu.VMEM((kv_local, total, hdim), BF16),
            pltpu.VMEM((kv_local, total, hdim), BF16),
            pltpu.VMEM((kv_local, hdim, total), BF16),
            pltpu.VMEM((kv_local, hdim, total), BF16),
            pltpu.VMEM((kv_local, tlen, hdim), F32),
            pltpu.VMEM((kv_local, tlen, hdim), F32),
            pltpu.SemaphoreType.DMA((cites,)),
        ],
        compiler_params=params(40),
        cost_estimate=cost(kv_local, nseg, block, 3 * total, hdim),
    )(scalar(table), q, do, own, arrived)


def settle_kernel(cites, table_ref, got_ref, out_ref, total, turned, sems):
    ntraj, nhead, per, dlen_local, hdim = got_ref.shape
    docs_dev = out_ref.shape[0]
    places = [table_ref[2 * cites + t] for t in range(ntraj)]
    stores = []
    for d in range(docs_dev):
        total[d] = jnp.zeros_like(total[d])
        for t in range(ntraj):

            @pl.when(places[t] == d)
            def _():
                total[d] += got_ref[t].astype(F32)

        turned[d] = jnp.swapaxes(total[d].reshape(nhead * per, dlen_local, hdim), 0, 1)
        stores.append(pltpu.make_async_copy(turned.at[d], out_ref.at[d], sems.at[d]))
        stores[-1].start()
    for store in stores:
        store.wait()


def settle(table, cites, got, docs_dev):
    _, nhead, per, dlen_local, hdim = got.shape
    return pl.pallas_call(
        functools.partial(settle_kernel, cites),
        out_shape=jax.ShapeDtypeStruct((docs_dev, dlen_local, nhead * per, hdim), F32),
        in_specs=[SMEM, VMEM],
        out_specs=HBM,
        scratch_shapes=[
            pltpu.VMEM((docs_dev, nhead, per, dlen_local, hdim), F32),
            pltpu.VMEM((docs_dev, dlen_local, nhead * per, hdim), F32),
            pltpu.SemaphoreType.DMA((docs_dev,)),
        ],
        compiler_params=params(32),
    )(scalar(table), near(got))


def body(queries, traj_kv, grad_out, doc_kv, citations, doc_slot, visible_from):
    nhead = lax.axis_size("head")
    ndp = lax.axis_size("dp")
    tlen, heads_local, hdim = queries.shape
    kv_local = traj_kv.shape[1]
    group = heads_local // kv_local
    docs_dev, dlen_local = doc_kv.shape[:2]
    per = kv_local * 2
    cites = citations.shape[1]
    outgoing, table = pack(citations.T, doc_slot, visible_from, doc_kv, nhead)
    arrived = lax.all_to_all(outgoing, ("dp", "head"), split_axis=0, concat_axis=0, tiled=True)
    arrived = arrived.reshape(ndp, nhead, per, dlen_local, hdim)

    def by_kv(x):
        x = x.reshape(tlen, kv_local, group, hdim).transpose(1, 0, 2, 3)
        return x.reshape(kv_local, tlen // SEG, SEG * group, hdim)

    def by_token(x):
        x = x.reshape(kv_local, tlen, group, hdim).transpose(1, 0, 2, 3)
        return x.reshape(tlen, heads_local, hdim)

    q = by_kv(queries)
    do = by_kv(grad_out)
    own = traj_kv.transpose(1, 2, 0, 3)
    part = attend_docs(table, cites, q, do, own, arrived)
    part, q, do, arrived = lax.optimization_barrier((part, q, do, arrived))
    got = lax.all_to_all(
        part.reshape(outgoing.shape), ("dp", "head"), split_axis=0, concat_axis=0, tiled=True
    )
    attended, d_queries, d_own = attend_rest(table, cites, q, do, own, arrived)
    d_doc = settle(table, cites, got.reshape(ndp, nhead, per, dlen_local, hdim), docs_dev)
    return (
        by_token(attended),
        by_token(d_queries),
        d_own.transpose(2, 0, 1, 3),
        d_doc.reshape(docs_dev, dlen_local, nhead * kv_local, 2, hdim),
    )


def solution(mesh):
    in_specs = (
        P("dp", "head", None),
        P("dp", "head", None, None),
        P("dp", "head", None),
        P("dp", "head", None, None, None),
        P(),
        P(),
        P("dp", None),
    )
    out_specs = (
        P("dp", "head", None),
        P("dp", "head", None),
        P("dp", "head", None, None),
        P("dp", "head", None, None, None),
    )
    return jax.shard_map(body, mesh=mesh, in_specs=in_specs, out_specs=out_specs, check_vma=False)
```

```python
import functools
import math

import jax
import jax.numpy as jnp
from jax import lax
from jax.experimental import pallas as pl
from jax.experimental.pallas import tpu as pltpu
from jax.sharding import PartitionSpec as P

SEG = 64
BF16 = jnp.bfloat16
F32 = jnp.float32
NT = (((1,), (1,)), ((), ()))
NN = (((1,), (0,)), ((), ()))
SMEM = pl.BlockSpec(memory_space=pltpu.SMEM)
VMEM = pl.BlockSpec(memory_space=pltpu.VMEM)
HBM = pl.BlockSpec(memory_space=pltpu.HBM)


def dot(a, b, dims):
    return lax.dot_general(a, b, dims, preferred_element_type=F32)


def params(megabytes):
    return pltpu.CompilerParams(vmem_limit_bytes=megabytes * 1024 * 1024)


def cost(*shape):
    flops = 2 * math.prod(shape)
    return pl.CostEstimate(flops=flops, bytes_accessed=8 * 1024 * 1024, transcendentals=0)


def near(x):
    return pltpu.with_memory_space_constraint(x, pltpu.VMEM)


def scalar(x):
    return pltpu.with_memory_space_constraint(x, pltpu.SMEM)


def place_of(cit_ref, slot_ref, t, cites, docs_dev, me):
    place = jnp.int32(-1)
    for c in range(cites):
        slot = slot_ref[cit_ref[c, t]]
        place = jnp.where(lax.div(slot, docs_dev) == me, lax.rem(slot, docs_dev), place)
    return place


def pack_kernel(
    cit_hbm, slot_hbm, vis_hbm, doc_ref, out_ref, table_ref,
    cit_ref, slot_ref, vis_ref, held, turned, in_sems, out_sems,
):
    me = lax.axis_index("dp")
    cites, ntraj = cit_ref.shape
    docs_dev = doc_ref.shape[0]
    scalars = [
        pltpu.make_async_copy(cit_hbm, cit_ref, in_sems.at[docs_dev]),
        pltpu.make_async_copy(slot_hbm, slot_ref, in_sems.at[docs_dev + 1]),
        pltpu.make_async_copy(vis_hbm, vis_ref, in_sems.at[docs_dev + 2]),
    ]
    for load in scalars:
        load.start()
    loads = [pltpu.make_async_copy(doc_ref.at[d], held.at[d], in_sems.at[d]) for d in range(docs_dev)]
    for load in loads:
        load.start()
    for load in scalars:
        load.wait()
    places = [place_of(cit_ref, slot_ref, t, cites, docs_dev, me) for t in range(ntraj)]
    stores = []
    for t in range(ntraj):
        source = turned.at[jnp.maximum(places[t], 0)]
        stores.append(pltpu.make_async_copy(source, out_ref.at[t], out_sems.at[t]))
        table_ref[2 * cites + t] = places[t]
    for c in range(cites):
        table_ref[c] = lax.div(slot_ref[cit_ref[c, me]], docs_dev)
        table_ref[cites + c] = vis_ref[0, c]
    for d in range(docs_dev):
        loads[d].wait()
        turned[d] = jnp.swapaxes(held[d].astype(F32), 0, 1).astype(BF16)
        for t in range(ntraj):
            pl.when(places[t] == d)(stores[t].start)
    for t in range(ntraj):
        pl.when(places[t] >= 0)(stores[t].wait)


def pack(cit, doc_slot, visible_from, doc_kv, nhead):
    docs_dev, dlen_local, kv, two, hdim = doc_kv.shape
    cites, ntraj = cit.shape
    rows = kv * two
    out, table = pl.pallas_call(
        pack_kernel,
        out_shape=(
            pltpu.HBM((ntraj, rows, dlen_local, hdim), BF16),
            pltpu.SMEM((2 * cites + ntraj,), jnp.int32),
        ),
        in_specs=[HBM, HBM, HBM, HBM],
        out_specs=(HBM, SMEM),
        scratch_shapes=[
            pltpu.SMEM(cit.shape, jnp.int32),
            pltpu.SMEM(doc_slot.shape, jnp.int32),
            pltpu.SMEM(visible_from.shape, jnp.int32),
            pltpu.VMEM((docs_dev, dlen_local, rows, hdim), BF16),
            pltpu.VMEM((docs_dev, rows, dlen_local, hdim), BF16),
            pltpu.SemaphoreType.DMA((docs_dev + 3,)),
            pltpu.SemaphoreType.DMA((ntraj,)),
        ],
        compiler_params=params(60),
    )(cit, doc_slot, visible_from, doc_kv.reshape(docs_dev, dlen_local, rows, hdim))
    return out.reshape(ntraj * nhead, rows // nhead, dlen_local, hdim), table


def own_seen(seg, tlen, lanes, group):
    key = lax.broadcasted_iota(jnp.int32, (tlen, lanes), 0)
    token = seg * SEG + lax.broadcasted_iota(jnp.int32, (tlen, lanes), 1) // group
    return key <= token


def seg_spec(kv_local, rows, columns):
    return pl.BlockSpec((kv_local, 1, rows, columns), lambda s: (0, s, 0, 0))


def docs_kernel(
    cites, rate, scale, depth,
    table_ref, q_ref, do_ref, own_ref, arr_ref,
    part_hbm,
    keys, vals, vals_t, own_t, dkey, dval, part_ref, sems,
):
    kv_local, nseg, lanes, hdim = q_ref.shape
    _, nhead, _, dlen_local, _ = arr_ref.shape
    dlen = nhead * dlen_local
    owners = [table_ref[c] for c in range(cites)]
    for g in range(kv_local):
        own_t[g] = own_ref[g, 1].T
        for c in range(cites):
            rows = pl.ds(c * dlen, dlen)
            keys[g, rows, :] = arr_ref[owners[c], :, 2 * g].reshape(dlen, hdim)
            value = arr_ref[owners[c], :, 2 * g + 1].reshape(dlen, hdim)
            vals[g, rows, :] = value
            vals_t[g, :, rows] = value.T

    def add(ref, g, seg, term):
        ref[g] = term if seg == 0 else ref[g] + term

    def stages(g, seg):
        q = q_ref[g, seg]
        do = do_ref[g, seg]
        before = seg * SEG
        score = dot(keys[g], q, NT)
        own = dot(own_ref[g, 0, : before + SEG], q, NT)
        yield
        seen = own_seen(0, SEG, lanes, lanes // SEG)
        edge = jnp.where(seen, own[before:], -jnp.inf)
        own = jnp.concatenate([own[:before], edge], 0) if before else edge
        own_top = jnp.max(own, axis=0, keepdims=True)
        own_weight = jnp.exp2((own - own_top) * rate)
        top = own_top
        tops = []
        sums = []
        weights = []
        for c in range(cites):
            part = score[c * dlen : (c + 1) * dlen]
            doc_top = jnp.max(part, axis=0, keepdims=True)
            weights.append(jnp.exp2((part - doc_top) * rate))
            sums.append(jnp.sum(weights[-1], axis=0, keepdims=True))
            tops.append(jnp.where(table_ref[cites + c] <= seg, doc_top, -jnp.inf))
            top = jnp.maximum(top, tops[-1])
        own_factor = jnp.exp2((own_top - top) * rate)
        factors = [jnp.exp2((t - top) * rate) for t in tops]
        total = jnp.sum(own_weight, axis=0, keepdims=True) * own_factor
        for f, s in zip(factors, sums):
            total = total + f * s
        inverse = 1.0 / total
        prob = jnp.concatenate([(w * (f * inverse)).astype(BF16) for w, f in zip(weights, factors)], 0)
        own_prob = (own_weight * (own_factor * inverse)).astype(BF16)
        yield
        out = dot(own_t[g, :, : before + SEG], own_prob, NN) + dot(vals_t[g], prob, NN)
        add(dval, g, seg, dot(prob, do, NN))
        out = out.astype(BF16)
        yield
        delta = jnp.sum(do.T.astype(F32) * out.astype(F32), axis=0, keepdims=True)
        dprob = dot(vals[g], do, NT)
        dscore = (prob.astype(F32) * (dprob - delta)).astype(BF16)
        yield
        add(dkey, g, seg, dot(dscore, q, NN))
        yield
        if seg == nseg - 1:
            give(g)

    shape = (nhead, dlen_local, hdim)
    copies = []

    def give(g):
        pair = pl.ds(2 * g, 2)
        for c in range(cites):
            rows = pl.ds(c * dlen, dlen)
            part_ref[c, :, 2 * g] = (dkey[g, rows, :] * scale).astype(BF16).reshape(shape)
            part_ref[c, :, 2 * g + 1] = dval[g, rows, :].astype(BF16).reshape(shape)
        for c in range(cites):
            source = part_ref.at[c, :, pair]
            target = part_hbm.at[owners[c], :, pair]
            copies.append(pltpu.make_async_copy(source, target, sems.at[g * cites + c]))
            copies[-1].start()

    waiting = [stages(g, seg) for seg in range(nseg) for g in range(kv_local)]
    active = []
    while waiting or active:
        if waiting and len(active) < depth:
            active.append(waiting.pop(0))
        active = [item for item in active if next(item, "end") != "end"]
    for copy in copies:
        copy.wait()


def attend_docs(table, cites, q, do, own, arrived):
    kv_local, nseg, block, hdim = q.shape
    _, nhead, per, dlen_local, _ = arrived.shape
    ndoc = cites * nhead * dlen_local
    rate = 1.0 / (math.sqrt(hdim) * math.log(2.0))
    depth = 5 if ndoc <= 512 else 1
    return pl.pallas_call(
        functools.partial(docs_kernel, cites, rate, 1.0 / math.sqrt(hdim), depth),
        out_shape=pltpu.HBM(arrived.shape, BF16),
        in_specs=[SMEM, VMEM, VMEM, VMEM, VMEM],
        out_specs=HBM,
        scratch_shapes=[
            pltpu.VMEM((kv_local, ndoc, hdim), BF16),
            pltpu.VMEM((kv_local, ndoc, hdim), BF16),
            pltpu.VMEM((kv_local, hdim, ndoc), BF16),
            pltpu.VMEM((kv_local, hdim, own.shape[2]), BF16),
            pltpu.VMEM((kv_local, ndoc, hdim), F32),
            pltpu.VMEM((kv_local, ndoc, hdim), F32),
            pltpu.VMEM((cites,) + arrived.shape[1:], BF16),
            pltpu.SemaphoreType.DMA((kv_local * cites,)),
        ],
        compiler_params=params(40),
        cost_estimate=cost(kv_local, nseg, block, ndoc, hdim, 5),
    )(scalar(table), near(q), near(do), near(own), near(arrived))


def rest_kernel(
    group, rate, scale,
    table_ref, q_ref, do_ref, own_ref, arr_ref,
    o_ref, dq_ref, down_ref,
    held, keys, vals, keys_t, vals_t, dkey, dval, sems,
):
    seg = pl.program_id(0)
    last = pl.num_programs(0) - 1
    kv_local, _, lanes, hdim = q_ref.shape
    cites, nhead, _, dlen_local, _ = held.shape
    dlen = nhead * dlen_local
    ndoc = cites * dlen
    tlen = own_ref.shape[2]

    def fetch(c):
        return pltpu.make_async_copy(arr_ref.at[table_ref[c]], held.at[c], sems.at[c])

    @pl.when(seg == 0)
    def _():
        for c in range(cites):
            fetch(c).start()
        dkey[...] = jnp.zeros_like(dkey)
        dval[...] = jnp.zeros_like(dval)
        for c in range(cites):
            fetch(c).wait()
            rows = pl.ds(c * dlen, dlen)
            for g in range(kv_local):
                keys[g, rows, :] = held[c, :, 2 * g].reshape(dlen, hdim)
                vals[g, rows, :] = held[c, :, 2 * g + 1].reshape(dlen, hdim)
        for g in range(kv_local):
            keys[g, ndoc:, :] = own_ref[g, 0]
            vals[g, ndoc:, :] = own_ref[g, 1]
            keys_t[g] = keys[g].T
            vals_t[g] = vals[g].T

    seen = own_seen(seg, tlen, lanes, group)
    for g in range(kv_local):
        q = q_ref[g, 0]
        do = do_ref[g, 0]
        score = dot(keys[g], q, NT)
        parts = [
            jnp.where(table_ref[cites + c] <= seg, score[c * dlen : (c + 1) * dlen], -jnp.inf)
            for c in range(cites)
        ]
        parts.append(jnp.where(seen, score[ndoc:], -jnp.inf))
        score = jnp.concatenate(parts, 0)
        weight = jnp.exp2((score - jnp.max(score, axis=0, keepdims=True)) * rate)
        prob = weight * (1.0 / jnp.sum(weight, axis=0, keepdims=True))
        prob16 = prob.astype(BF16)
        out = dot(vals_t[g], prob16, NN).astype(BF16)
        o_ref[g, 0] = out.T
        delta = jnp.sum(do.T.astype(F32) * out.astype(F32), axis=0, keepdims=True)
        dprob = dot(vals[g], do, NT)
        dscore = (prob * (dprob - delta)).astype(BF16)
        dkey[g] += dot(dscore[ndoc:], q, NN)
        dval[g] += dot(prob16[ndoc:], do, NN)
        dq_ref[g, 0] = (dot(keys_t[g], dscore, NN) * scale).astype(BF16).T

    @pl.when(seg == last)
    def _():
        down_ref[:, 0] = (dkey[...] * scale).astype(BF16)
        down_ref[:, 1] = dval[...].astype(BF16)


def attend_rest(table, cites, q, do, own, arrived):
    kv_local, nseg, block, hdim = q.shape
    tlen = own.shape[2]
    _, nhead, per, dlen_local, _ = arrived.shape
    total = cites * nhead * dlen_local + tlen
    row_spec = seg_spec(kv_local, block, hdim)
    whole_own = pl.BlockSpec(own.shape, lambda s: (0, 0, 0, 0))
    rate = 1.0 / (math.sqrt(hdim) * math.log(2.0))
    return pl.pallas_call(
        functools.partial(rest_kernel, block // SEG, rate, 1.0 / math.sqrt(hdim)),
        grid=(nseg,),
        out_shape=(
            jax.ShapeDtypeStruct(q.shape, BF16),
            jax.ShapeDtypeStruct(q.shape, BF16),
            jax.ShapeDtypeStruct(own.shape, BF16),
        ),
        in_specs=[SMEM, row_spec, row_spec, whole_own, HBM],
        out_specs=(row_spec, row_spec, whole_own),
        scratch_shapes=[
            pltpu.VMEM((cites, nhead, per, dlen_local, hdim), BF16),
            pltpu.VMEM((kv_local, total, hdim), BF16),
            pltpu.VMEM((kv_local, total, hdim), BF16),
            pltpu.VMEM((kv_local, hdim, total), BF16),
            pltpu.VMEM((kv_local, hdim, total), BF16),
            pltpu.VMEM((kv_local, tlen, hdim), F32),
            pltpu.VMEM((kv_local, tlen, hdim), F32),
            pltpu.SemaphoreType.DMA((cites,)),
        ],
        compiler_params=params(40),
        cost_estimate=cost(kv_local, nseg, block, 3 * total, hdim),
    )(scalar(table), q, do, own, arrived)


def settle_kernel(cites, table_ref, got_ref, out_ref, total, turned, sems):
    ntraj, nhead, per, dlen_local, hdim = got_ref.shape
    docs_dev = out_ref.shape[0]
    places = [table_ref[2 * cites + t] for t in range(ntraj)]
    stores = []
    for d in range(docs_dev):
        total[d] = jnp.zeros_like(total[d])
        for t in range(ntraj):

            @pl.when(places[t] == d)
            def _():
                total[d] += got_ref[t].astype(F32)

        turned[d] = jnp.swapaxes(total[d].reshape(nhead * per, dlen_local, hdim), 0, 1)
        stores.append(pltpu.make_async_copy(turned.at[d], out_ref.at[d], sems.at[d]))
        stores[-1].start()
    for store in stores:
        store.wait()


def settle(table, cites, got, docs_dev):
    _, nhead, per, dlen_local, hdim = got.shape
    return pl.pallas_call(
        functools.partial(settle_kernel, cites),
        out_shape=jax.ShapeDtypeStruct((docs_dev, dlen_local, nhead * per, hdim), F32),
        in_specs=[SMEM, VMEM],
        out_specs=HBM,
        scratch_shapes=[
            pltpu.VMEM((docs_dev, nhead, per, dlen_local, hdim), F32),
            pltpu.VMEM((docs_dev, dlen_local, nhead * per, hdim), F32),
            pltpu.SemaphoreType.DMA((docs_dev,)),
        ],
        compiler_params=params(32),
    )(scalar(table), near(got))


def body(queries, traj_kv, grad_out, doc_kv, citations, doc_slot, visible_from):
    nhead = lax.axis_size("head")
    ndp = lax.axis_size("dp")
    tlen, heads_local, hdim = queries.shape
    kv_local = traj_kv.shape[1]
    group = heads_local // kv_local
    docs_dev, dlen_local = doc_kv.shape[:2]
    per = kv_local * 2
    cites = citations.shape[1]
    outgoing, table = pack(citations.T, doc_slot, visible_from, doc_kv, nhead)
    arrived = lax.all_to_all(outgoing, ("dp", "head"), split_axis=0, concat_axis=0, tiled=True)
    arrived = arrived.reshape(ndp, nhead, per, dlen_local, hdim)

    def by_kv(x):
        x = x.reshape(tlen, kv_local, group, hdim).transpose(1, 0, 2, 3)
        return x.reshape(kv_local, tlen // SEG, SEG * group, hdim)

    def by_token(x):
        x = x.reshape(kv_local, tlen, group, hdim).transpose(1, 0, 2, 3)
        return x.reshape(tlen, heads_local, hdim)

    q = by_kv(queries)
    do = by_kv(grad_out)
    own = traj_kv.transpose(1, 2, 0, 3)
    part = attend_docs(table, cites, q, do, own, arrived)
    part, q, do, arrived = lax.optimization_barrier((part, q, do, arrived))
    got = lax.all_to_all(
        part.reshape(outgoing.shape), ("dp", "head"), split_axis=0, concat_axis=0, tiled=True
    )
    attended, d_queries, d_own = attend_rest(table, cites, q, do, own, arrived)
    d_doc = settle(table, cites, got.reshape(ndp, nhead, per, dlen_local, hdim), docs_dev)
    return (
        by_token(attended),
        by_token(d_queries),
        d_own.transpose(2, 0, 1, 3),
        d_doc.reshape(docs_dev, dlen_local, nhead * kv_local, 2, hdim),
    )


def solution(mesh):
    in_specs = (
        P("dp", "head", None),
        P("dp", "head", None, None),
        P("dp", "head", None),
        P("dp", "head", None, None, None),
        P(),
        P(),
        P("dp", None),
    )
    out_specs = (
        P("dp", "head", None),
        P("dp", "head", None),
        P("dp", "head", None, None),
        P("dp", "head", None, None, None),
    )
    return jax.shard_map(body, mesh=mesh, in_specs=in_specs, out_specs=out_specs, check_vma=False)
```

```python
import functools
import math

import jax
import jax.numpy as jnp
from jax import lax
from jax.experimental import pallas as pl
from jax.experimental.pallas import tpu as pltpu
from jax.sharding import PartitionSpec as P

SEG = 64
BF16 = jnp.bfloat16
F32 = jnp.float32
NT = (((1,), (1,)), ((), ()))
NN = (((1,), (0,)), ((), ()))
SMEM = pl.BlockSpec(memory_space=pltpu.SMEM)
VMEM = pl.BlockSpec(memory_space=pltpu.VMEM)
HBM = pl.BlockSpec(memory_space=pltpu.HBM)


def dot(a, b, dims):
    return lax.dot_general(a, b, dims, preferred_element_type=F32)


def params(megabytes):
    return pltpu.CompilerParams(vmem_limit_bytes=megabytes * 1024 * 1024)


def cost(*shape):
    flops = 2 * math.prod(shape)
    return pl.CostEstimate(flops=flops, bytes_accessed=8 * 1024 * 1024, transcendentals=0)


def near(x):
    return pltpu.with_memory_space_constraint(x, pltpu.VMEM)


def scalar(x):
    return pltpu.with_memory_space_constraint(x, pltpu.SMEM)


def place_of(cit_ref, slot_ref, t, cites, docs_dev, me):
    place = jnp.int32(-1)
    for c in range(cites):
        slot = slot_ref[cit_ref[c, t]]
        place = jnp.where(lax.div(slot, docs_dev) == me, lax.rem(slot, docs_dev), place)
    return place


def pack_kernel(
    cit_hbm, slot_hbm, vis_hbm, doc_ref, out_ref, table_ref,
    cit_ref, slot_ref, vis_ref, held, turned, in_sems, out_sems,
):
    me = lax.axis_index("dp")
    cites, ntraj = cit_ref.shape
    docs_dev = doc_ref.shape[0]
    scalars = [
        pltpu.make_async_copy(cit_hbm, cit_ref, in_sems.at[docs_dev]),
        pltpu.make_async_copy(slot_hbm, slot_ref, in_sems.at[docs_dev + 1]),
        pltpu.make_async_copy(vis_hbm, vis_ref, in_sems.at[docs_dev + 2]),
    ]
    for load in scalars:
        load.start()
    loads = [pltpu.make_async_copy(doc_ref.at[d], held.at[d], in_sems.at[d]) for d in range(docs_dev)]
    for load in loads:
        load.start()
    for load in scalars:
        load.wait()
    places = [place_of(cit_ref, slot_ref, t, cites, docs_dev, me) for t in range(ntraj)]
    stores = []
    for t in range(ntraj):
        source = turned.at[jnp.maximum(places[t], 0)]
        stores.append(pltpu.make_async_copy(source, out_ref.at[t], out_sems.at[t]))
        table_ref[2 * cites + t] = places[t]
    for c in range(cites):
        table_ref[c] = lax.div(slot_ref[cit_ref[c, me]], docs_dev)
        table_ref[cites + c] = vis_ref[0, c]
    for d in range(docs_dev):
        loads[d].wait()
        turned[d] = jnp.swapaxes(held[d].astype(F32), 0, 1).astype(BF16)
        for t in range(ntraj):
            pl.when(places[t] == d)(stores[t].start)
    for t in range(ntraj):
        pl.when(places[t] >= 0)(stores[t].wait)


def pack(cit, doc_slot, visible_from, doc_kv, nhead):
    docs_dev, dlen_local, kv, two, hdim = doc_kv.shape
    cites, ntraj = cit.shape
    rows = kv * two
    out, table = pl.pallas_call(
        pack_kernel,
        out_shape=(
            pltpu.HBM((ntraj, rows, dlen_local, hdim), BF16),
            pltpu.SMEM((2 * cites + ntraj,), jnp.int32),
        ),
        in_specs=[HBM, HBM, HBM, HBM],
        out_specs=(HBM, SMEM),
        scratch_shapes=[
            pltpu.SMEM(cit.shape, jnp.int32),
            pltpu.SMEM(doc_slot.shape, jnp.int32),
            pltpu.SMEM(visible_from.shape, jnp.int32),
            pltpu.VMEM((docs_dev, dlen_local, rows, hdim), BF16),
            pltpu.VMEM((docs_dev, rows, dlen_local, hdim), BF16),
            pltpu.SemaphoreType.DMA((docs_dev + 3,)),
            pltpu.SemaphoreType.DMA((ntraj,)),
        ],
        compiler_params=params(60),
    )(cit, doc_slot, visible_from, doc_kv.reshape(docs_dev, dlen_local, rows, hdim))
    return out.reshape(ntraj * nhead, rows // nhead, dlen_local, hdim), table


def own_seen(seg, tlen, lanes, group):
    key = lax.broadcasted_iota(jnp.int32, (tlen, lanes), 0)
    token = seg * SEG + lax.broadcasted_iota(jnp.int32, (tlen, lanes), 1) // group
    return key <= token


def seg_spec(kv_local, rows, columns):
    return pl.BlockSpec((kv_local, 1, rows, columns), lambda s: (0, s, 0, 0))


def docs_kernel(
    cites, rate, scale, depth,
    table_ref, q_ref, do_ref, own_ref, arr_ref,
    part_hbm,
    keys, vals, vals_t, dkey, dval, part_ref, sems,
):
    kv_local, nseg, lanes, hdim = q_ref.shape
    _, nhead, _, dlen_local, _ = arr_ref.shape
    dlen = nhead * dlen_local
    ndoc = cites * dlen
    owners = [table_ref[c] for c in range(cites)]
    for g in range(kv_local):
        keys[g, ndoc:, :] = own_ref[g, 0]
        vals_t[g, :, ndoc:] = own_ref[g, 1].T
        for c in range(cites):
            rows = pl.ds(c * dlen, dlen)
            keys[g, rows, :] = arr_ref[owners[c], :, 2 * g].reshape(dlen, hdim)
            value = arr_ref[owners[c], :, 2 * g + 1].reshape(dlen, hdim)
            vals[g, rows, :] = value
            vals_t[g, :, rows] = value.T

    def add(ref, g, seg, term):
        ref[g] = term if seg == 0 else ref[g] + term

    def stages(g, seg):
        q = q_ref[g, seg]
        do = do_ref[g, seg]
        before = seg * SEG
        used = ndoc + before + SEG
        score = dot(keys[g, :used], q, NT)
        own = score[ndoc:]
        yield
        seen = own_seen(0, SEG, lanes, lanes // SEG)
        edge = jnp.where(seen, own[before:], -jnp.inf)
        own = jnp.concatenate([own[:before], edge], 0) if before else edge
        own_top = jnp.max(own, axis=0, keepdims=True)
        own_weight = jnp.exp2((own - own_top) * rate)
        top = own_top
        tops = []
        sums = []
        weights = []
        for c in range(cites):
            part = score[c * dlen : (c + 1) * dlen]
            doc_top = jnp.max(part, axis=0, keepdims=True)
            weights.append(jnp.exp2((part - doc_top) * rate))
            sums.append(jnp.sum(weights[-1], axis=0, keepdims=True))
            tops.append(jnp.where(table_ref[cites + c] <= seg, doc_top, -jnp.inf))
            top = jnp.maximum(top, tops[-1])
        own_factor = jnp.exp2((own_top - top) * rate)
        factors = [jnp.exp2((t - top) * rate) for t in tops]
        total = jnp.sum(own_weight, axis=0, keepdims=True) * own_factor
        for f, s in zip(factors, sums):
            total = total + f * s
        inverse = 1.0 / total
        prob = jnp.concatenate([(w * (f * inverse)).astype(BF16) for w, f in zip(weights, factors)], 0)
        own_prob = (own_weight * (own_factor * inverse)).astype(BF16)
        seen_prob = jnp.concatenate([prob, own_prob], 0)
        yield
        out = dot(vals_t[g, :, :used], seen_prob, NN)
        add(dval, g, seg, dot(prob, do, NN))
        out = out.astype(BF16)
        yield
        delta = jnp.sum(do.T.astype(F32) * out.astype(F32), axis=0, keepdims=True)
        dprob = dot(vals[g], do, NT)
        dscore = (prob.astype(F32) * (dprob - delta)).astype(BF16)
        yield
        add(dkey, g, seg, dot(dscore, q, NN))
        yield
        if seg == nseg - 1:
            give(g)

    shape = (nhead, dlen_local, hdim)
    copies = []

    def give(g):
        pair = pl.ds(2 * g, 2)
        for c in range(cites):
            rows = pl.ds(c * dlen, dlen)
            part_ref[c, :, 2 * g] = (dkey[g, rows, :] * scale).astype(BF16).reshape(shape)
            part_ref[c, :, 2 * g + 1] = dval[g, rows, :].astype(BF16).reshape(shape)
        for c in range(cites):
            source = part_ref.at[c, :, pair]
            target = part_hbm.at[owners[c], :, pair]
            copies.append(pltpu.make_async_copy(source, target, sems.at[g * cites + c]))
            copies[-1].start()

    waiting = [stages(g, seg) for seg in range(nseg) for g in range(kv_local)]
    active = []
    while waiting or active:
        if waiting and len(active) < depth:
            active.append(waiting.pop(0))
        active = [item for item in active if next(item, "end") != "end"]
    for copy in copies:
        copy.wait()


def attend_docs(table, cites, q, do, own, arrived):
    kv_local, nseg, block, hdim = q.shape
    _, nhead, per, dlen_local, _ = arrived.shape
    ndoc = cites * nhead * dlen_local
    rate = 1.0 / (math.sqrt(hdim) * math.log(2.0))
    depth = 5 if ndoc <= 512 else 1
    return pl.pallas_call(
        functools.partial(docs_kernel, cites, rate, 1.0 / math.sqrt(hdim), depth),
        out_shape=pltpu.HBM(arrived.shape, BF16),
        in_specs=[SMEM, VMEM, VMEM, VMEM, VMEM],
        out_specs=HBM,
        scratch_shapes=[
            pltpu.VMEM((kv_local, ndoc + own.shape[2], hdim), BF16),
            pltpu.VMEM((kv_local, ndoc, hdim), BF16),
            pltpu.VMEM((kv_local, hdim, ndoc + own.shape[2]), BF16),
            pltpu.VMEM((kv_local, ndoc, hdim), F32),
            pltpu.VMEM((kv_local, ndoc, hdim), F32),
            pltpu.VMEM((cites,) + arrived.shape[1:], BF16),
            pltpu.SemaphoreType.DMA((kv_local * cites,)),
        ],
        compiler_params=params(40),
        cost_estimate=cost(kv_local, nseg, block, ndoc, hdim, 5),
    )(scalar(table), near(q), near(do), near(own), near(arrived))


def rest_kernel(
    group, rate, scale,
    table_ref, q_ref, do_ref, own_ref, arr_ref,
    o_ref, dq_ref, down_ref,
    held, keys, vals, keys_t, vals_t, dkey, dval, sems,
):
    seg = pl.program_id(0)
    last = pl.num_programs(0) - 1
    kv_local, _, lanes, hdim = q_ref.shape
    cites, nhead, _, dlen_local, _ = held.shape
    dlen = nhead * dlen_local
    ndoc = cites * dlen
    tlen = own_ref.shape[2]

    def fetch(c):
        return pltpu.make_async_copy(arr_ref.at[table_ref[c]], held.at[c], sems.at[c])

    @pl.when(seg == 0)
    def _():
        for c in range(cites):
            fetch(c).start()
        dkey[...] = jnp.zeros_like(dkey)
        dval[...] = jnp.zeros_like(dval)
        for c in range(cites):
            fetch(c).wait()
            rows = pl.ds(c * dlen, dlen)
            for g in range(kv_local):
                keys[g, rows, :] = held[c, :, 2 * g].reshape(dlen, hdim)
                vals[g, rows, :] = held[c, :, 2 * g + 1].reshape(dlen, hdim)
        for g in range(kv_local):
            keys[g, ndoc:, :] = own_ref[g, 0]
            vals[g, ndoc:, :] = own_ref[g, 1]
            keys_t[g] = keys[g].T
            vals_t[g] = vals[g].T

    seen = own_seen(seg, tlen, lanes, group)
    for g in range(kv_local):
        q = q_ref[g, 0]
        do = do_ref[g, 0]
        score = dot(keys[g], q, NT)
        parts = [
            jnp.where(table_ref[cites + c] <= seg, score[c * dlen : (c + 1) * dlen], -jnp.inf)
            for c in range(cites)
        ]
        parts.append(jnp.where(seen, score[ndoc:], -jnp.inf))
        score = jnp.concatenate(parts, 0)
        weight = jnp.exp2((score - jnp.max(score, axis=0, keepdims=True)) * rate)
        prob = weight * (1.0 / jnp.sum(weight, axis=0, keepdims=True))
        prob16 = prob.astype(BF16)
        out = dot(vals_t[g], prob16, NN).astype(BF16)
        o_ref[g, 0] = out.T
        delta = jnp.sum(do.T.astype(F32) * out.astype(F32), axis=0, keepdims=True)
        dprob = dot(vals[g], do, NT)
        dscore = (prob * (dprob - delta)).astype(BF16)
        dkey[g] += dot(dscore[ndoc:], q, NN)
        dval[g] += dot(prob16[ndoc:], do, NN)
        dq_ref[g, 0] = (dot(keys_t[g], dscore, NN) * scale).astype(BF16).T

    @pl.when(seg == last)
    def _():
        down_ref[:, 0] = (dkey[...] * scale).astype(BF16)
        down_ref[:, 1] = dval[...].astype(BF16)


def attend_rest(table, cites, q, do, own, arrived):
    kv_local, nseg, block, hdim = q.shape
    tlen = own.shape[2]
    _, nhead, per, dlen_local, _ = arrived.shape
    total = cites * nhead * dlen_local + tlen
    row_spec = seg_spec(kv_local, block, hdim)
    whole_own = pl.BlockSpec(own.shape, lambda s: (0, 0, 0, 0))
    rate = 1.0 / (math.sqrt(hdim) * math.log(2.0))
    return pl.pallas_call(
        functools.partial(rest_kernel, block // SEG, rate, 1.0 / math.sqrt(hdim)),
        grid=(nseg,),
        out_shape=(
            jax.ShapeDtypeStruct(q.shape, BF16),
            jax.ShapeDtypeStruct(q.shape, BF16),
            jax.ShapeDtypeStruct(own.shape, BF16),
        ),
        in_specs=[SMEM, row_spec, row_spec, whole_own, HBM],
        out_specs=(row_spec, row_spec, whole_own),
        scratch_shapes=[
            pltpu.VMEM((cites, nhead, per, dlen_local, hdim), BF16),
            pltpu.VMEM((kv_local, total, hdim), BF16),
            pltpu.VMEM((kv_local, total, hdim), BF16),
            pltpu.VMEM((kv_local, hdim, total), BF16),
            pltpu.VMEM((kv_local, hdim, total), BF16),
            pltpu.VMEM((kv_local, tlen, hdim), F32),
            pltpu.VMEM((kv_local, tlen, hdim), F32),
            pltpu.SemaphoreType.DMA((cites,)),
        ],
        compiler_params=params(40),
        cost_estimate=cost(kv_local, nseg, block, 3 * total, hdim),
    )(scalar(table), q, do, own, arrived)


def settle_kernel(cites, table_ref, got_ref, out_ref, total, turned, sems):
    ntraj, nhead, per, dlen_local, hdim = got_ref.shape
    docs_dev = out_ref.shape[0]
    places = [table_ref[2 * cites + t] for t in range(ntraj)]
    stores = []
    for d in range(docs_dev):
        total[d] = jnp.zeros_like(total[d])
        for t in range(ntraj):

            @pl.when(places[t] == d)
            def _():
                total[d] += got_ref[t].astype(F32)

        turned[d] = jnp.swapaxes(total[d].reshape(nhead * per, dlen_local, hdim), 0, 1)
        stores.append(pltpu.make_async_copy(turned.at[d], out_ref.at[d], sems.at[d]))
        stores[-1].start()
    for store in stores:
        store.wait()


def settle(table, cites, got, docs_dev):
    _, nhead, per, dlen_local, hdim = got.shape
    return pl.pallas_call(
        functools.partial(settle_kernel, cites),
        out_shape=jax.ShapeDtypeStruct((docs_dev, dlen_local, nhead * per, hdim), F32),
        in_specs=[SMEM, VMEM],
        out_specs=HBM,
        scratch_shapes=[
            pltpu.VMEM((docs_dev, nhead, per, dlen_local, hdim), F32),
            pltpu.VMEM((docs_dev, dlen_local, nhead * per, hdim), F32),
            pltpu.SemaphoreType.DMA((docs_dev,)),
        ],
        compiler_params=params(32),
    )(scalar(table), near(got))


def body(queries, traj_kv, grad_out, doc_kv, citations, doc_slot, visible_from):
    nhead = lax.axis_size("head")
    ndp = lax.axis_size("dp")
    tlen, heads_local, hdim = queries.shape
    kv_local = traj_kv.shape[1]
    group = heads_local // kv_local
    docs_dev, dlen_local = doc_kv.shape[:2]
    per = kv_local * 2
    cites = citations.shape[1]
    outgoing, table = pack(citations.T, doc_slot, visible_from, doc_kv, nhead)
    arrived = lax.all_to_all(outgoing, ("dp", "head"), split_axis=0, concat_axis=0, tiled=True)
    arrived = arrived.reshape(ndp, nhead, per, dlen_local, hdim)

    def by_kv(x):
        x = x.reshape(tlen, kv_local, group, hdim).transpose(1, 0, 2, 3)
        return x.reshape(kv_local, tlen // SEG, SEG * group, hdim)

    def by_token(x):
        x = x.reshape(kv_local, tlen, group, hdim).transpose(1, 0, 2, 3)
        return x.reshape(tlen, heads_local, hdim)

    q = by_kv(queries)
    do = by_kv(grad_out)
    own = traj_kv.transpose(1, 2, 0, 3)
    part = attend_docs(table, cites, q, do, own, arrived)
    part, q, do, arrived = lax.optimization_barrier((part, q, do, arrived))
    got = lax.all_to_all(
        part.reshape(outgoing.shape), ("dp", "head"), split_axis=0, concat_axis=0, tiled=True
    )
    attended, d_queries, d_own = attend_rest(table, cites, q, do, own, arrived)
    d_doc = settle(table, cites, got.reshape(ndp, nhead, per, dlen_local, hdim), docs_dev)
    return (
        by_token(attended),
        by_token(d_queries),
        d_own.transpose(2, 0, 1, 3),
        d_doc.reshape(docs_dev, dlen_local, nhead * kv_local, 2, hdim),
    )


def solution(mesh):
    in_specs = (
        P("dp", "head", None),
        P("dp", "head", None, None),
        P("dp", "head", None),
        P("dp", "head", None, None, None),
        P(),
        P(),
        P("dp", None),
    )
    out_specs = (
        P("dp", "head", None),
        P("dp", "head", None),
        P("dp", "head", None, None),
        P("dp", "head", None, None, None),
    )
    return jax.shard_map(body, mesh=mesh, in_specs=in_specs, out_specs=out_specs, check_vma=False)
```

```python
import functools
import math

import jax
import jax.numpy as jnp
from jax import lax
from jax.experimental import pallas as pl
from jax.experimental.pallas import tpu as pltpu
from jax.sharding import PartitionSpec as P

SEG = 64
BF16 = jnp.bfloat16
F32 = jnp.float32
NT = (((1,), (1,)), ((), ()))
NN = (((1,), (0,)), ((), ()))
SMEM = pl.BlockSpec(memory_space=pltpu.SMEM)
VMEM = pl.BlockSpec(memory_space=pltpu.VMEM)
HBM = pl.BlockSpec(memory_space=pltpu.HBM)


def dot(a, b, dims):
    return lax.dot_general(a, b, dims, preferred_element_type=F32)


def params(megabytes):
    return pltpu.CompilerParams(vmem_limit_bytes=megabytes * 1024 * 1024)


def cost(*shape):
    flops = 2 * math.prod(shape)
    return pl.CostEstimate(flops=flops, bytes_accessed=8 * 1024 * 1024, transcendentals=0)


def near(x):
    return pltpu.with_memory_space_constraint(x, pltpu.VMEM)


def scalar(x):
    return pltpu.with_memory_space_constraint(x, pltpu.SMEM)


def place_of(cit_ref, slot_ref, t, cites, docs_dev, me):
    place = jnp.int32(-1)
    for c in range(cites):
        slot = slot_ref[cit_ref[c, t]]
        place = jnp.where(lax.div(slot, docs_dev) == me, lax.rem(slot, docs_dev), place)
    return place


def pack_kernel(
    cit_hbm, slot_hbm, vis_hbm, doc_ref, out_ref, table_ref,
    cit_ref, slot_ref, vis_ref, held, turned, in_sems, out_sems,
):
    me = lax.axis_index("dp")
    cites, ntraj = cit_ref.shape
    docs_dev = doc_ref.shape[0]
    scalars = [
        pltpu.make_async_copy(cit_hbm, cit_ref, in_sems.at[docs_dev]),
        pltpu.make_async_copy(slot_hbm, slot_ref, in_sems.at[docs_dev + 1]),
        pltpu.make_async_copy(vis_hbm, vis_ref, in_sems.at[docs_dev + 2]),
    ]
    for load in scalars:
        load.start()
    loads = [pltpu.make_async_copy(doc_ref.at[d], held.at[d], in_sems.at[d]) for d in range(docs_dev)]
    for load in loads:
        load.start()
    for load in scalars:
        load.wait()
    places = [place_of(cit_ref, slot_ref, t, cites, docs_dev, me) for t in range(ntraj)]
    stores = []
    for t in range(ntraj):
        source = turned.at[jnp.maximum(places[t], 0)]
        stores.append(pltpu.make_async_copy(source, out_ref.at[t], out_sems.at[t]))
        table_ref[2 * cites + t] = places[t]
    for c in range(cites):
        table_ref[c] = lax.div(slot_ref[cit_ref[c, me]], docs_dev)
        table_ref[cites + c] = vis_ref[0, c]
    for d in range(docs_dev):
        loads[d].wait()
        turned[d] = jnp.swapaxes(held[d].astype(F32), 0, 1).astype(BF16)
        for t in range(ntraj):
            pl.when(places[t] == d)(stores[t].start)
    for t in range(ntraj):
        pl.when(places[t] >= 0)(stores[t].wait)


def pack(cit, doc_slot, visible_from, doc_kv, nhead):
    docs_dev, dlen_local, kv, two, hdim = doc_kv.shape
    cites, ntraj = cit.shape
    rows = kv * two
    out, table = pl.pallas_call(
        pack_kernel,
        out_shape=(
            pltpu.HBM((ntraj, rows, dlen_local, hdim), BF16),
            pltpu.SMEM((2 * cites + ntraj,), jnp.int32),
        ),
        in_specs=[HBM, HBM, HBM, HBM],
        out_specs=(HBM, SMEM),
        scratch_shapes=[
            pltpu.SMEM(cit.shape, jnp.int32),
            pltpu.SMEM(doc_slot.shape, jnp.int32),
            pltpu.SMEM(visible_from.shape, jnp.int32),
            pltpu.VMEM((docs_dev, dlen_local, rows, hdim), BF16),
            pltpu.VMEM((docs_dev, rows, dlen_local, hdim), BF16),
            pltpu.SemaphoreType.DMA((docs_dev + 3,)),
            pltpu.SemaphoreType.DMA((ntraj,)),
        ],
        compiler_params=params(60),
    )(cit, doc_slot, visible_from, doc_kv.reshape(docs_dev, dlen_local, rows, hdim))
    return out.reshape(ntraj * nhead, rows // nhead, dlen_local, hdim), table


def own_seen(seg, tlen, lanes, group):
    key = lax.broadcasted_iota(jnp.int32, (tlen, lanes), 0)
    token = seg * SEG + lax.broadcasted_iota(jnp.int32, (tlen, lanes), 1) // group
    return key <= token


def seg_spec(kv_local, rows, columns):
    return pl.BlockSpec((kv_local, 1, rows, columns), lambda s: (0, s, 0, 0))


def docs_kernel(
    cites, rate, scale, depth,
    table_ref, q_ref, do_ref, own_ref, arr_ref,
    part_hbm,
    keys, vals, vals_t, dkey, dval, part_ref, sems,
):
    kv_local, nseg, lanes, hdim = q_ref.shape
    _, nhead, _, dlen_local, _ = arr_ref.shape
    dlen = nhead * dlen_local
    ndoc = cites * dlen
    owners = [table_ref[c] for c in range(cites)]
    for g in range(kv_local):
        keys[g, ndoc:, :] = own_ref[g, 0]
        vals_t[g, :, ndoc:] = own_ref[g, 1].T
        for c in range(cites):
            rows = pl.ds(c * dlen, dlen)
            keys[g, rows, :] = arr_ref[owners[c], :, 2 * g].reshape(dlen, hdim)
            value = arr_ref[owners[c], :, 2 * g + 1].reshape(dlen, hdim)
            vals[g, rows, :] = value
            vals_t[g, :, rows] = value.T

    shape = (nhead, dlen_local, hdim)
    copies = []

    def add(ref, g, seg, term, row, factor):
        total = term if seg == 0 else ref[g] + term
        if seg < nseg - 1:
            ref[g] = total
            return
        total = (total * factor).astype(BF16)
        for c in range(cites):
            part_ref[c, :, 2 * g + row] = total[c * dlen : (c + 1) * dlen].reshape(shape)

    def stages(g, seg):
        q = q_ref[g, seg]
        do = do_ref[g, seg]
        before = seg * SEG
        used = ndoc + before + SEG
        score = dot(keys[g, :used], q, NT)
        own = score[ndoc:]
        yield
        seen = own_seen(0, SEG, lanes, lanes // SEG)
        edge = jnp.where(seen, own[before:], -jnp.inf)
        own = jnp.concatenate([own[:before], edge], 0) if before else edge
        own_top = jnp.max(own, axis=0, keepdims=True)
        own_weight = jnp.exp2((own - own_top) * rate)
        top = own_top
        tops = []
        sums = []
        weights = []
        for c in range(cites):
            part = score[c * dlen : (c + 1) * dlen]
            doc_top = jnp.max(part, axis=0, keepdims=True)
            weights.append(jnp.exp2((part - doc_top) * rate))
            sums.append(jnp.sum(weights[-1], axis=0, keepdims=True))
            tops.append(jnp.where(table_ref[cites + c] <= seg, doc_top, -jnp.inf))
            top = jnp.maximum(top, tops[-1])
        own_factor = jnp.exp2((own_top - top) * rate)
        factors = [jnp.exp2((t - top) * rate) for t in tops]
        total = jnp.sum(own_weight, axis=0, keepdims=True) * own_factor
        for f, s in zip(factors, sums):
            total = total + f * s
        inverse = 1.0 / total
        prob = jnp.concatenate([(w * (f * inverse)).astype(BF16) for w, f in zip(weights, factors)], 0)
        own_prob = (own_weight * (own_factor * inverse)).astype(BF16)
        seen_prob = jnp.concatenate([prob, own_prob], 0)
        yield
        out = dot(vals_t[g, :, :used], seen_prob, NN)
        add(dval, g, seg, dot(prob, do, NN), 1, 1.0)
        out = out.astype(BF16)
        yield
        delta = jnp.sum(do.T.astype(F32) * out.astype(F32), axis=0, keepdims=True)
        dprob = dot(vals[g], do, NT)
        dscore = (prob.astype(F32) * (dprob - delta)).astype(BF16)
        yield
        add(dkey, g, seg, dot(dscore, q, NN), 0, scale)
        yield
        if seg == nseg - 1:
            give(g)

    def give(g):
        pair = pl.ds(2 * g, 2)
        for c in range(cites):
            source = part_ref.at[c, :, pair]
            target = part_hbm.at[owners[c], :, pair]
            copies.append(pltpu.make_async_copy(source, target, sems.at[g * cites + c]))
            copies[-1].start()

    waiting = [stages(g, seg) for seg in range(nseg) for g in range(kv_local)]
    active = []
    while waiting or active:
        if waiting and len(active) < depth:
            active.append(waiting.pop(0))
        active = [item for item in active if next(item, "end") != "end"]
    for copy in copies:
        copy.wait()


def attend_docs(table, cites, q, do, own, arrived):
    kv_local, nseg, block, hdim = q.shape
    _, nhead, per, dlen_local, _ = arrived.shape
    ndoc = cites * nhead * dlen_local
    rate = 1.0 / (math.sqrt(hdim) * math.log(2.0))
    depth = 5 if ndoc <= 512 else 1
    return pl.pallas_call(
        functools.partial(docs_kernel, cites, rate, 1.0 / math.sqrt(hdim), depth),
        out_shape=pltpu.HBM(arrived.shape, BF16),
        in_specs=[SMEM, VMEM, VMEM, VMEM, VMEM],
        out_specs=HBM,
        scratch_shapes=[
            pltpu.VMEM((kv_local, ndoc + own.shape[2], hdim), BF16),
            pltpu.VMEM((kv_local, ndoc, hdim), BF16),
            pltpu.VMEM((kv_local, hdim, ndoc + own.shape[2]), BF16),
            pltpu.VMEM((kv_local, ndoc, hdim), F32),
            pltpu.VMEM((kv_local, ndoc, hdim), F32),
            pltpu.VMEM((cites,) + arrived.shape[1:], BF16),
            pltpu.SemaphoreType.DMA((kv_local * cites,)),
        ],
        compiler_params=params(40),
        cost_estimate=cost(kv_local, nseg, block, ndoc, hdim, 5),
    )(scalar(table), near(q), near(do), near(own), near(arrived))


def rest_kernel(
    group, rate, scale,
    table_ref, q_ref, do_ref, own_ref, arr_ref,
    o_ref, dq_ref, down_ref,
    held, keys, vals, keys_t, vals_t, dkey, dval, sems,
):
    seg = pl.program_id(0)
    last = pl.num_programs(0) - 1
    kv_local, _, lanes, hdim = q_ref.shape
    cites, nhead, _, dlen_local, _ = held.shape
    dlen = nhead * dlen_local
    ndoc = cites * dlen
    tlen = own_ref.shape[2]

    def fetch(c):
        return pltpu.make_async_copy(arr_ref.at[table_ref[c]], held.at[c], sems.at[c])

    @pl.when(seg == 0)
    def _():
        for c in range(cites):
            fetch(c).start()
        dkey[...] = jnp.zeros_like(dkey)
        dval[...] = jnp.zeros_like(dval)
        for c in range(cites):
            fetch(c).wait()
            rows = pl.ds(c * dlen, dlen)
            for g in range(kv_local):
                keys[g, rows, :] = held[c, :, 2 * g].reshape(dlen, hdim)
                vals[g, rows, :] = held[c, :, 2 * g + 1].reshape(dlen, hdim)
        for g in range(kv_local):
            keys[g, ndoc:, :] = own_ref[g, 0]
            vals[g, ndoc:, :] = own_ref[g, 1]
            keys_t[g] = keys[g].T
            vals_t[g] = vals[g].T

    seen = own_seen(seg, tlen, lanes, group)
    for g in range(kv_local):
        q = q_ref[g, 0]
        do = do_ref[g, 0]
        score = dot(keys[g], q, NT)
        parts = [
            jnp.where(table_ref[cites + c] <= seg, score[c * dlen : (c + 1) * dlen], -jnp.inf)
            for c in range(cites)
        ]
        parts.append(jnp.where(seen, score[ndoc:], -jnp.inf))
        score = jnp.concatenate(parts, 0)
        weight = jnp.exp2((score - jnp.max(score, axis=0, keepdims=True)) * rate)
        prob = weight * (1.0 / jnp.sum(weight, axis=0, keepdims=True))
        prob16 = prob.astype(BF16)
        out = dot(vals_t[g], prob16, NN).astype(BF16)
        o_ref[g, 0] = out.T
        delta = jnp.sum(do.T.astype(F32) * out.astype(F32), axis=0, keepdims=True)
        dprob = dot(vals[g], do, NT)
        dscore = (prob * (dprob - delta)).astype(BF16)
        dkey[g] += dot(dscore[ndoc:], q, NN)
        dval[g] += dot(prob16[ndoc:], do, NN)
        dq_ref[g, 0] = (dot(keys_t[g], dscore, NN) * scale).astype(BF16).T

    @pl.when(seg == last)
    def _():
        down_ref[:, 0] = (dkey[...] * scale).astype(BF16)
        down_ref[:, 1] = dval[...].astype(BF16)


def attend_rest(table, cites, q, do, own, arrived):
    kv_local, nseg, block, hdim = q.shape
    tlen = own.shape[2]
    _, nhead, per, dlen_local, _ = arrived.shape
    total = cites * nhead * dlen_local + tlen
    row_spec = seg_spec(kv_local, block, hdim)
    whole_own = pl.BlockSpec(own.shape, lambda s: (0, 0, 0, 0))
    rate = 1.0 / (math.sqrt(hdim) * math.log(2.0))
    return pl.pallas_call(
        functools.partial(rest_kernel, block // SEG, rate, 1.0 / math.sqrt(hdim)),
        grid=(nseg,),
        out_shape=(
            jax.ShapeDtypeStruct(q.shape, BF16),
            jax.ShapeDtypeStruct(q.shape, BF16),
            jax.ShapeDtypeStruct(own.shape, BF16),
        ),
        in_specs=[SMEM, row_spec, row_spec, whole_own, HBM],
        out_specs=(row_spec, row_spec, whole_own),
        scratch_shapes=[
            pltpu.VMEM((cites, nhead, per, dlen_local, hdim), BF16),
            pltpu.VMEM((kv_local, total, hdim), BF16),
            pltpu.VMEM((kv_local, total, hdim), BF16),
            pltpu.VMEM((kv_local, hdim, total), BF16),
            pltpu.VMEM((kv_local, hdim, total), BF16),
            pltpu.VMEM((kv_local, tlen, hdim), F32),
            pltpu.VMEM((kv_local, tlen, hdim), F32),
            pltpu.SemaphoreType.DMA((cites,)),
        ],
        compiler_params=params(40),
        cost_estimate=cost(kv_local, nseg, block, 3 * total, hdim),
    )(scalar(table), q, do, own, arrived)


def settle_kernel(cites, table_ref, got_ref, out_ref, total, turned, sems):
    ntraj, nhead, per, dlen_local, hdim = got_ref.shape
    docs_dev = out_ref.shape[0]
    places = [table_ref[2 * cites + t] for t in range(ntraj)]
    stores = []
    for d in range(docs_dev):
        total[d] = jnp.zeros_like(total[d])
        for t in range(ntraj):

            @pl.when(places[t] == d)
            def _():
                total[d] += got_ref[t].astype(F32)

        turned[d] = jnp.swapaxes(total[d].reshape(nhead * per, dlen_local, hdim), 0, 1)
        stores.append(pltpu.make_async_copy(turned.at[d], out_ref.at[d], sems.at[d]))
        stores[-1].start()
    for store in stores:
        store.wait()


def settle(table, cites, got, docs_dev):
    _, nhead, per, dlen_local, hdim = got.shape
    return pl.pallas_call(
        functools.partial(settle_kernel, cites),
        out_shape=jax.ShapeDtypeStruct((docs_dev, dlen_local, nhead * per, hdim), F32),
        in_specs=[SMEM, VMEM],
        out_specs=HBM,
        scratch_shapes=[
            pltpu.VMEM((docs_dev, nhead, per, dlen_local, hdim), F32),
            pltpu.VMEM((docs_dev, dlen_local, nhead * per, hdim), F32),
            pltpu.SemaphoreType.DMA((docs_dev,)),
        ],
        compiler_params=params(32),
    )(scalar(table), near(got))


def body(queries, traj_kv, grad_out, doc_kv, citations, doc_slot, visible_from):
    nhead = lax.axis_size("head")
    ndp = lax.axis_size("dp")
    tlen, heads_local, hdim = queries.shape
    kv_local = traj_kv.shape[1]
    group = heads_local // kv_local
    docs_dev, dlen_local = doc_kv.shape[:2]
    per = kv_local * 2
    cites = citations.shape[1]
    outgoing, table = pack(citations.T, doc_slot, visible_from, doc_kv, nhead)
    arrived = lax.all_to_all(outgoing, ("dp", "head"), split_axis=0, concat_axis=0, tiled=True)
    arrived = arrived.reshape(ndp, nhead, per, dlen_local, hdim)

    def by_kv(x):
        x = x.reshape(tlen, kv_local, group, hdim).transpose(1, 0, 2, 3)
        return x.reshape(kv_local, tlen // SEG, SEG * group, hdim)

    def by_token(x):
        x = x.reshape(kv_local, tlen, group, hdim).transpose(1, 0, 2, 3)
        return x.reshape(tlen, heads_local, hdim)

    q = by_kv(queries)
    do = by_kv(grad_out)
    own = traj_kv.transpose(1, 2, 0, 3)
    part = attend_docs(table, cites, q, do, own, arrived)
    part, q, do, arrived = lax.optimization_barrier((part, q, do, arrived))
    got = lax.all_to_all(
        part.reshape(outgoing.shape), ("dp", "head"), split_axis=0, concat_axis=0, tiled=True
    )
    attended, d_queries, d_own = attend_rest(table, cites, q, do, own, arrived)
    d_doc = settle(table, cites, got.reshape(ndp, nhead, per, dlen_local, hdim), docs_dev)
    return (
        by_token(attended),
        by_token(d_queries),
        d_own.transpose(2, 0, 1, 3),
        d_doc.reshape(docs_dev, dlen_local, nhead * kv_local, 2, hdim),
    )


def solution(mesh):
    in_specs = (
        P("dp", "head", None),
        P("dp", "head", None, None),
        P("dp", "head", None),
        P("dp", "head", None, None, None),
        P(),
        P(),
        P("dp", None),
    )
    out_specs = (
        P("dp", "head", None),
        P("dp", "head", None),
        P("dp", "head", None, None),
        P("dp", "head", None, None, None),
    )
    return jax.shard_map(body, mesh=mesh, in_specs=in_specs, out_specs=out_specs, check_vma=False)
```
